512 devices in a mesh: section: 128 (over z, y, core), dp: 4 (over x).
Axes of the slice: x: 4, y: 4, z: 16, core: 2. Of those that a mesh axis runs over, the one named last changes fastest.
Arguments:
- features: bfloat16 [4, 32768, 128], P('dp', 'section'), may hold values from -6 to 6
- grad_out: bfloat16 [4, 32768, 512], P('dp', 'section'), may hold values from -0.015625 to 0.015625
- w_first: bfloat16 [128, 512], replicated, may hold values from -0.5 to 0.5
- w_second: bfloat16 [512, 512], replicated, may hold values from -0.25 to 0.25
- tile_values: bfloat16 [4, 1024, 128, 128], P('dp', 'section'), may hold values from -0.25 to 0.25
- tile_rows: int32 [4, 1024], P('dp', 'section'), may hold values from 0 to 1, as said below
- tile_cols: int32 [4, 1024], P('dp', 'section'), may hold values from 0 to 5, as said below
- tile_count: int32 [4, 128], P('dp', 'section'), may hold values from 2 to 8, as said below
Outputs:
- grad_w1_t: float32 [512, 128], P(('section', 'dp'))
- grad_w2: float32 [512, 512], P(('section', 'dp'))
The draws below stay inside these ranges and needn't reach their ends.
Inputs may be any that keep to these rules, and one draw needn't show every extreme that they name: Within one device, the pairs (tile_rows, tile_cols) of its slots are all different. `tile_cols`: blocks 0 to 1 are the previous device's, 2 to 3 the own, the rest the next device's. `tile_count`: in every graph batch some device uses all 8 slots; slots at or above a device's count hold no tile.
All inputs are finite; a program needn't handle non-finite values.
Results may differ from the reference program's by a relative error of at most 0.013.
Values may be sent and summed in bfloat16 or wider, within the bound.
No kernel may reach another device: no remote copies, remote signals or barrier semaphores. Data moves between devices by JAX's collectives and lax.ppermute only.
A program may use at most 64 MiB of HBM per device.

```python
import jax
import jax.numpy as jnp
from jax import lax

D = 512
F = 128
TILE = 128
TILES_DEV = 8
BLK_DEV = 2
NODES = 32768
MICRO = 4
N_SECTION = 128


def tile_pairs(key):
    streams = jax.random.split(jax.random.fold_in(key, 11), MICRO * N_SECTION)
    chosen = jax.vmap(lambda stream: jax.random.permutation(stream, 3 * BLK_DEV * BLK_DEV)[:TILES_DEV])(streams)
    return chosen.reshape(MICRO, N_SECTION * TILES_DEV).astype(jnp.int32)


def draw_tile_rows(key, part):
    chosen = tile_pairs(key)
    return (chosen // (3 * BLK_DEV)).astype(jnp.int32)


def draw_tile_cols(key, part):
    chosen = tile_pairs(key)
    return (chosen % (3 * BLK_DEV)).astype(jnp.int32)


def draw_tile_count(key, part):
    key = jax.random.fold_in(key, 3)
    first_key, second_key = jax.random.split(key)
    counts = jax.random.randint(first_key, (MICRO, N_SECTION), TILES_DEV // 3, TILES_DEV + 1)
    fullest = jax.random.randint(second_key, (MICRO,), 0, N_SECTION)
    places = jnp.arange(N_SECTION, dtype=jnp.int32)[None, :]
    return jnp.where(places == fullest[:, None], TILES_DEV, counts).astype(jnp.int32)


def steps_of(key, shape, cuts, smallest, largest):
    def one(dim, parts):
        steps = jax.random.uniform(jax.random.fold_in(jax.random.fold_in(key, 6), dim), (parts,), jnp.float32, smallest / len(cuts), largest / len(cuts))
        return jnp.repeat(jnp.exp(steps), shape[dim] // parts).reshape((-1,) + (1,) * (len(shape) - dim - 1))

    gain = one(*cuts[0])
    for cut in cuts[1:]:
        gain = gain * one(*cut)
    return gain


def noise(key, dims, deviation, bound, shards=(), kind=jnp.bfloat16):
    level = steps_of(key, dims, shards, -0.22, 0.18) if shards else 1.0
    drawn = jax.random.normal(key, dims, jnp.float32) * deviation * level
    return jnp.minimum(jnp.maximum(drawn, -bound), bound).astype(kind)


def setup_inputs(seed: int = 0) -> dict:
    splits = jax.random.split(jax.random.key(seed), 9)
    features = noise(splits[0], (MICRO, NODES, F), 1.0, 6.0, ((0, 4), (1, 128)))
    grad_out = noise(splits[1], (MICRO, NODES, D), (NODES * MICRO) ** -0.5, 0.015625, ((0, 4), (1, 128)))
    w_first = noise(splits[2], (F, D), F ** -0.5, 0.5)
    w_second = noise(splits[3], (D, D), D ** -0.5, 0.25)
    tile_values = noise(splits[4], (MICRO, N_SECTION * TILES_DEV, TILE, TILE), (TILE * TILES_DEV // BLK_DEV) ** -0.5, 0.25, ((0, 4), (1, 128)))
    tile_rows = draw_tile_rows(jax.random.fold_in(splits[8], 71), 0)
    tile_cols = draw_tile_cols(jax.random.fold_in(splits[8], 71), 0)
    tile_count = draw_tile_count(jax.random.fold_in(splits[8], 71), 0)
    return {"features": features, "grad_out": grad_out, "w_first": w_first, "w_second": w_second, "tile_values": tile_values, "tile_rows": tile_rows, "tile_cols": tile_cols, "tile_count": tile_count}


def gelu_pair(inputs_in):
    values, pullback = jax.vjp(lambda entry: jax.nn.gelu(entry, approximate=True), inputs_in)
    slopes = pullback(jnp.ones_like(inputs_in))[0]
    return (values, slopes)

def forward_sum(hidden, values, row_ids, col_ids, live_count):
    columns = hidden.shape[1]
    blocks = hidden.reshape(N_SECTION * BLK_DEV, TILE, columns)
    padding = jnp.zeros((BLK_DEV, TILE, columns), hidden.dtype)
    padded = jnp.concatenate([padding, blocks, padding], axis=0)
    values = values.reshape(N_SECTION, TILES_DEV, TILE, TILE)
    row_ids = row_ids.reshape(N_SECTION, TILES_DEV)
    col_ids = col_ids.reshape(N_SECTION, TILES_DEV)

    def per_device(pack):
        device, tile_vals, tile_r, tile_c, number = pack
        window = lax.dynamic_slice_in_dim(padded, (device * BLK_DEV).astype(jnp.int32), 3 * BLK_DEV, 0)
        picked = window[tile_c]
        product = jnp.einsum('tab,tbw->taw', tile_vals.astype(jnp.float32), picked.astype(jnp.float32))
        live_slot = jnp.arange(TILES_DEV, dtype=jnp.int32) < number
        onehot = ((tile_r[None, :] == jnp.arange(BLK_DEV, dtype=jnp.int32)[:, None]) & live_slot[None, :]).astype(jnp.float32)
        return jnp.einsum('rt,taw->raw', onehot, product, precision=lax.Precision.HIGHEST)
    devices = jnp.arange(N_SECTION, dtype=jnp.int32)
    pieces = lax.map(per_device, (devices, values, row_ids, col_ids, live_count))
    return pieces.reshape(NODES, columns)

def backward_sum(grads, values, row_ids, col_ids, live_count):
    columns = grads.shape[1]
    blocks = grads.reshape(N_SECTION, BLK_DEV, TILE, columns)
    values = values.reshape(N_SECTION, TILES_DEV, TILE, TILE)
    row_ids = row_ids.reshape(N_SECTION, TILES_DEV)
    col_ids = col_ids.reshape(N_SECTION, TILES_DEV)

    def per_device(pack):
        own_blocks, tile_vals, tile_r, tile_c, number = pack
        picked = own_blocks[tile_r]
        product = jnp.einsum('tab,taw->tbw', tile_vals.astype(jnp.float32), picked.astype(jnp.float32))
        live_slot = jnp.arange(TILES_DEV, dtype=jnp.int32) < number
        onehot = ((tile_c[None, :] == jnp.arange(3 * BLK_DEV, dtype=jnp.int32)[:, None]) & live_slot[None, :]).astype(jnp.float32)
        return jnp.einsum('ct,tbw->cbw', onehot, product, precision=lax.Precision.HIGHEST)
    pieces = lax.map(per_device, (blocks, values, row_ids, col_ids, live_count))
    zeros_row = jnp.zeros((1, BLK_DEV, TILE, columns), jnp.float32)
    total = pieces[:, BLK_DEV:2 * BLK_DEV]
    total = total + jnp.concatenate([pieces[1:, :BLK_DEV], zeros_row], axis=0)
    total = total + jnp.concatenate([zeros_row, pieces[:-1, 2 * BLK_DEV:]], axis=0)
    return total.reshape(NODES, columns)

def reference(features, grad_out, w_first, w_second, tile_values, tile_rows, tile_cols, tile_count):
    grad_first = jnp.zeros((D, F), jnp.float32)
    grad_second = jnp.zeros((D, D), jnp.float32)
    for micro in range(MICRO):
        tile_args = (tile_values[micro], tile_rows[micro], tile_cols[micro], tile_count[micro])
        agg1 = forward_sum(features[micro], *tile_args).astype(jnp.bfloat16)
        pre1 = jnp.dot(agg1, w_first, preferred_element_type=jnp.float32)
        hid1, slope1 = gelu_pair(pre1)
        hid1 = hid1.astype(jnp.bfloat16)
        agg2 = forward_sum(hid1, *tile_args).astype(jnp.bfloat16)
        pre2 = jnp.dot(agg2, w_second, preferred_element_type=jnp.float32)
        unused, slope2 = gelu_pair(pre2)
        dpre2 = (grad_out[micro].astype(jnp.float32) * slope2).astype(jnp.bfloat16)
        grad_second = grad_second + jnp.dot(agg2.T, dpre2, preferred_element_type=jnp.float32)
        dagg2 = jnp.dot(dpre2, w_second.T, preferred_element_type=jnp.float32).astype(jnp.bfloat16)
        dhid1 = backward_sum(dagg2, *tile_args)
        dpre1 = (dhid1 * slope1).astype(jnp.bfloat16)
        grad_first = grad_first + jnp.dot(dpre1.T, agg1, preferred_element_type=jnp.float32)
    return (grad_first, grad_second)
```

```python
import jax
import jax.numpy as jnp
import numpy as np
from jax import lax
from jax.experimental import pallas as pl
from jax.experimental.pallas import tpu as pltpu
from jax.sharding import Mesh
from jax.sharding import PartitionSpec as P

TILE = 128
SECTION = ("z", "y", "c")
PLANE = ("y", "c", "x")
SCALE = 0.7978845608028654
CUBIC = 0.044715
VMEM = pl.BlockSpec(memory_space=pltpu.VMEM)
SMEM = pl.BlockSpec(memory_space=pltpu.SMEM)


def fill_adjacency(rows_ref, cols_ref, count_ref, tiles_ref, adj_ref):
    adj_ref[...] = jnp.zeros_like(adj_ref)
    live = count_ref[0, 0]
    for slot in range(tiles_ref.shape[1]):

        @pl.when(slot < live)
        def _():
            row = pl.multiple_of(rows_ref[0, slot] * TILE, TILE)
            col = pl.multiple_of(cols_ref[0, slot] * TILE, TILE)
            adj_ref[pl.ds(row, TILE), pl.ds(col, TILE)] = tiles_ref[0, slot]


def dot(lhs, rhs, lhs_dim=1, rhs_dim=0):
    return lax.dot_general(
        lhs, rhs, (((lhs_dim,), (rhs_dim,)), ((), ())), preferred_element_type=jnp.float32
    )


def gelu_parts(v):
    square = v * v
    t = jnp.tanh(v * (SCALE + (SCALE * CUBIC) * square))
    half = 0.5 + 0.5 * t
    slope = half + (0.5 * v) * (1.0 - t * t) * (SCALE + (3.0 * SCALE * CUBIC) * square)
    return v * half, slope


def first_kernel(rows_ref, cols_ref, count_ref, low_ref, own_ref, high_ref, tiles_ref, out_ref, adj_ref):
    fill_adjacency(rows_ref, cols_ref, count_ref, tiles_ref, adj_ref)
    nodes = own_ref.shape[0]
    total = dot(adj_ref[:, nodes : 2 * nodes], own_ref[...])
    total += dot(adj_ref[:, :nodes], low_ref[...])
    total += dot(adj_ref[:, 2 * nodes :], high_ref[...])
    out_ref[...] = total.astype(jnp.bfloat16)


def second_kernel(
    rows_ref, cols_ref, count_ref, low_ref, own_ref, high_ref, tiles_ref, cot_ref, w1_ref, w2_ref,
    out_ref, adj_ref, agg_ref, hid_ref, slope_ref,
):
    fill_adjacency(rows_ref, cols_ref, count_ref, tiles_ref, adj_ref)
    nodes = own_ref.shape[0]
    hidden = w2_ref.shape[0]
    for part, ref in enumerate((low_ref, own_ref, high_ref)):
        place = pl.ds(part * nodes, nodes)
        agg_ref[place, :] = ref[...]
        pre1 = dot(ref[...], w1_ref[...])
        value, slope = gelu_parts(pre1)
        hid_ref[place, :] = value.astype(jnp.bfloat16)
        slope_ref[place, :] = slope
    agg2 = dot(adj_ref[...], hid_ref[...]).astype(jnp.bfloat16)
    pre2 = dot(agg2, w2_ref[...])
    unused, slope2 = gelu_parts(pre2)
    dpre2 = (cot_ref[0].astype(jnp.float32) * slope2).astype(jnp.bfloat16)
    dagg2 = dot(dpre2, w2_ref[...], 1, 1).astype(jnp.bfloat16)
    spread = dot(adj_ref[...], dagg2, 0, 0)
    dpre1 = (spread * slope_ref[...]).astype(jnp.bfloat16)
    second = dot(agg2, dpre2, 0, 0).astype(jnp.bfloat16)
    first = dot(dpre1, agg_ref[...], 0, 0).astype(jnp.bfloat16)
    groups, depth = out_ref.shape[0], out_ref.shape[1]
    target = lax.broadcasted_iota(jnp.int32, (hidden, hidden), 0)
    source = lax.broadcasted_iota(jnp.int32, (hidden, hidden), 1)
    wanted = (target % depth) * groups + target // depth
    order = (source == wanted).astype(jnp.bfloat16)
    features = first.shape[1]
    moved = dot(order, first).astype(jnp.bfloat16)
    out_ref[:, :, :features] = moved.reshape(groups, depth, features)
    moved = dot(order, second).astype(jnp.bfloat16)
    out_ref[:, :, features:] = moved.reshape(groups, depth, second.shape[1])


def plane_sum_kernel(in_ref, out_ref):
    total = in_ref[0].astype(jnp.float32)
    for source in range(1, in_ref.shape[0]):
        total += in_ref[source].astype(jnp.float32)
    out_ref[...] = jnp.zeros_like(out_ref)
    for piece in range(total.shape[1] // 128):
        out_ref[:, piece, :] = total[:, piece * 128 : (piece + 1) * 128]


def depth_sum_kernel(in_ref, first_ref, second_ref):
    total = jnp.sum(in_ref[...], axis=0)
    first_ref[...] = total[0:1, :]
    for piece in range(second_ref.shape[1] // 128):
        second_ref[:, piece * 128 : (piece + 1) * 128] = total[piece + 1 : piece + 2, :]


def shifted(block, distance):
    devices = range(lax.axis_size(SECTION))
    route = [(i, i + distance) for i in devices if i + distance in devices]
    return lax.ppermute(block, SECTION, route)


def body(features, grad_out, w_first, w_second, tile_values, tile_rows, tile_cols, tile_count):
    own = features[0]
    nodes, in_features = own.shape
    hidden = w_second.shape[0]
    depth = lax.axis_size("z")
    plane = lax.axis_size(PLANE)
    ids = (tile_rows, tile_cols, tile_count)
    adjacency = pltpu.VMEM((nodes, 3 * nodes), jnp.bfloat16)

    agg1 = pl.pallas_call(
        first_kernel,
        out_shape=jax.ShapeDtypeStruct((nodes, in_features), jnp.bfloat16),
        in_specs=[SMEM] * 3 + [VMEM] * 4,
        out_specs=VMEM,
        scratch_shapes=[adjacency],
        name="first_aggregation",
    )(*ids, shifted(own, 1), own, shifted(own, -1), tile_values)

    gradients = pl.pallas_call(
        second_kernel,
        out_shape=jax.ShapeDtypeStruct((plane, depth, in_features + hidden), jnp.bfloat16),
        in_specs=[SMEM] * 3 + [VMEM] * 7,
        out_specs=VMEM,
        scratch_shapes=[
            adjacency,
            pltpu.VMEM((3 * nodes, in_features), jnp.bfloat16),
            pltpu.VMEM((3 * nodes, hidden), jnp.bfloat16),
            pltpu.VMEM((3 * nodes, hidden), jnp.float32),
        ],
        compiler_params=pltpu.CompilerParams(vmem_limit_bytes=32 * 1024 * 1024),
        name="layers",
    )(*ids, shifted(agg1, 1), agg1, shifted(agg1, -1), tile_values, grad_out, w_first, w_second)

    gathered = lax.all_to_all(gradients, PLANE, 0, 0, tiled=True)
    partial = pl.pallas_call(
        plane_sum_kernel,
        out_shape=jax.ShapeDtypeStruct((depth, 8, 128), jnp.float32),
        in_specs=[VMEM],
        out_specs=VMEM,
        name="plane_sum",
    )(gathered)
    collected = lax.all_to_all(partial, "z", 0, 0, tiled=True)
    return pl.pallas_call(
        depth_sum_kernel,
        out_shape=(
            jax.ShapeDtypeStruct((1, in_features), jnp.float32),
            jax.ShapeDtypeStruct((1, hidden), jnp.float32),
        ),
        in_specs=[VMEM],
        out_specs=(VMEM, VMEM),
        name="depth_sum",
    )(collected)


def solution(mesh):
    fine = Mesh(mesh.devices.reshape(16, 4, 2, 4), ("z", "y", "c", "x"))
    placed = (
        P("x", SECTION, None),
        P("x", SECTION, None),
        P(),
        P(),
        P("x", SECTION, None, None),
        P("x", SECTION),
        P("x", SECTION),
        P("x", SECTION),
    )
    rows = ("z", "y", "c", "x")
    return jax.shard_map(
        body,
        mesh=fine,
        in_specs=placed,
        out_specs=(P(rows, None), P(rows, None)),
        check_vma=False,
    )
```

```python
import jax
import jax.numpy as jnp
from jax import lax
from jax.experimental import pallas as pl
from jax.experimental.pallas import tpu as pltpu
from jax.sharding import Mesh
from jax.sharding import PartitionSpec as P

TILE = 128
SECTION = ("z", "y", "c")
PLANE = ("y", "c", "x")
SCALE = 0.7978845608028654
CUBIC = 0.044715
VMEM = pl.BlockSpec(memory_space=pltpu.VMEM)
SMEM = pl.BlockSpec(memory_space=pltpu.SMEM)


def dot(lhs, rhs, lhs_dim=1, rhs_dim=0):
    return lax.dot_general(
        lhs, rhs, (((lhs_dim,), (rhs_dim,)), ((), ())), preferred_element_type=jnp.float32
    )


def gelu_parts(v):
    square = v * v
    t = jnp.tanh(v * (SCALE + (SCALE * CUBIC) * square))
    half = 0.5 + 0.5 * t
    slope = half + (0.5 * v) * (1.0 - t * t) * (SCALE + (3.0 * SCALE * CUBIC) * square)
    return v * half, slope


def adjacency_kernel(rows_ref, cols_ref, count_ref, odd_ref, tiles_ref, adj_ref):
    adj_ref[...] = jnp.zeros_like(adj_ref)
    live = count_ref[0, 0]
    odd = odd_ref[0]
    for slot in range(tiles_ref.shape[1]):

        @pl.when(slot < live)
        def _():
            row = pl.multiple_of(rows_ref[0, slot] * TILE, TILE)
            col = cols_ref[0, slot]
            side = col // 2
            part = jnp.where(odd == 1, 2 - side, side)
            col = pl.multiple_of((col - 2 * side) * TILE, TILE)
            adj_ref[part, pl.ds(row, TILE), pl.ds(col, TILE)] = tiles_ref[0, slot]


def layers_kernel(adj_ref, cross_ref, own_ref, other_ref, cot_ref, w1_ref, w2_ref, out_ref, slope_ref):
    hidden = w2_ref.shape[0]
    parts = (cross_ref, own_ref, other_ref)
    agg2 = None
    for part, ref in enumerate(parts):
        value, slope = gelu_parts(dot(ref[...], w1_ref[...]))
        slope_ref[part] = slope
        term = dot(adj_ref[part], value.astype(jnp.bfloat16))
        agg2 = term if agg2 is None else agg2 + term
    agg2 = agg2.astype(jnp.bfloat16)
    unused, slope2 = gelu_parts(dot(agg2, w2_ref[...]))
    dpre2 = (cot_ref[0].astype(jnp.float32) * slope2).astype(jnp.bfloat16)
    dagg2 = dot(dpre2, w2_ref[...], 1, 1).astype(jnp.bfloat16)
    first = None
    for part, ref in enumerate(parts):
        spread = dot(adj_ref[part], dagg2, 0, 0)
        dpre1 = (spread * slope_ref[part]).astype(jnp.bfloat16)
        term = dot(ref[...], dpre1, 0, 0)
        first = term if first is None else first + term
    first = first.astype(jnp.bfloat16)
    second = dot(agg2, dpre2, 0, 0).astype(jnp.bfloat16)
    groups, depth = out_ref.shape[0], out_ref.shape[1]
    target = lax.broadcasted_iota(jnp.int32, (hidden, hidden), 0)
    source = lax.broadcasted_iota(jnp.int32, (hidden, hidden), 1)
    wanted = (target % depth) * groups + target // depth
    order = (source == wanted).astype(jnp.bfloat16)
    features = first.shape[0]
    moved = dot(order, first, 1, 1).astype(jnp.bfloat16)
    out_ref[:, :, :features] = moved.reshape(groups, depth, features)
    moved = dot(order, second).astype(jnp.bfloat16)
    out_ref[:, :, features:] = moved.reshape(groups, depth, second.shape[1])


def cross_swap(block):
    count = lax.axis_size(SECTION)
    pairs = [(i, i + 1) for i in range(1, count - 1, 2)]
    return lax.ppermute(block, SECTION, pairs + [(j, i) for i, j in pairs])


def core_swap(block):
    return lax.ppermute(block, "c", [(0, 1), (1, 0)])


def body(features, grad_out, w_first, w_second, tile_values, tile_rows, tile_cols, tile_count):
    own = features[0]
    nodes, in_features = own.shape
    hidden = w_second.shape[0]
    depth = lax.axis_size("z")
    plane = lax.axis_size(PLANE)
    odd = lax.axis_index("c").astype(jnp.int32).reshape(1)

    cross = cross_swap(own)
    other = core_swap(own)
    adjacency = pl.pallas_call(
        adjacency_kernel,
        out_shape=jax.ShapeDtypeStruct((3, nodes, nodes), jnp.bfloat16),
        in_specs=[SMEM] * 4 + [VMEM],
        out_specs=VMEM,
        compiler_params=pltpu.CompilerParams(vmem_limit_bytes=4 * 1024 * 1024),
        name="adjacency",
    )(tile_rows, tile_cols, tile_count, odd, tile_values)
    near = dot(adjacency[1], own) + dot(adjacency[2], other)
    agg1 = (near + dot(adjacency[0], cross)).astype(jnp.bfloat16)

    gradients = pl.pallas_call(
        layers_kernel,
        out_shape=jax.ShapeDtypeStruct((plane, depth, in_features + hidden), jnp.bfloat16),
        in_specs=[VMEM] * 7,
        out_specs=VMEM,
        scratch_shapes=[pltpu.VMEM((3, nodes, hidden), jnp.float32)],
        compiler_params=pltpu.CompilerParams(vmem_limit_bytes=14 * 1024 * 1024),
        name="layers",
    )(adjacency, cross_swap(agg1), agg1, core_swap(agg1), grad_out, w_first, w_second)

    gathered = lax.all_to_all(gradients, PLANE, 0, 0, tiled=True)
    partial = jnp.sum(gathered.astype(jnp.float32), axis=0)
    partial = partial.reshape(depth, (in_features + hidden) // 128, 128)
    collected = lax.all_to_all(partial, "z", 0, 0, tiled=True)
    total = jnp.sum(collected, axis=0)
    first_rows = in_features // 128
    return total[:first_rows].reshape(1, in_features), total[first_rows:].reshape(1, hidden)


def solution(mesh):
    fine = Mesh(mesh.devices.reshape(16, 4, 2, 4), ("z", "y", "c", "x"))
    placed = (
        P("x", SECTION, None),
        P("x", SECTION, None),
        P(),
        P(),
        P("x", SECTION, None, None),
        P("x", SECTION),
        P("x", SECTION),
        P("x", SECTION),
    )
    rows = ("z", "y", "c", "x")
    return jax.shard_map(
        body,
        mesh=fine,
        in_specs=placed,
        out_specs=(P(rows, None), P(rows, None)),
        check_vma=False,
    )
```

```python
import functools

import jax
import jax.numpy as jnp
from jax import lax
from jax.experimental import pallas as pl
from jax.experimental.pallas import tpu as pltpu
from jax.sharding import Mesh
from jax.sharding import PartitionSpec as P

TILE = 128
SECTION = ("z", "y", "c")
PLANE = ("y", "c", "x")
SCALE = 0.7978845608028654
CUBIC = 0.044715
MIB = 1024 * 1024
VMEM = pl.BlockSpec(memory_space=pltpu.VMEM)
HBM = pl.BlockSpec(memory_space=pltpu.HBM)
SMEM = pl.BlockSpec(memory_space=pltpu.SMEM)


def dot(lhs, rhs, lhs_dim=1, rhs_dim=0):
    return lax.dot_general(
        lhs, rhs, (((lhs_dim,), (rhs_dim,)), ((), ())), preferred_element_type=jnp.float32
    )


def gelu_parts(v):
    square = v * v
    t = jnp.tanh(v * (SCALE + (SCALE * CUBIC) * square))
    half = 0.5 + 0.5 * t
    slope = half + (0.5 * v) * (1.0 - t * t) * (SCALE + (3.0 * SCALE * CUBIC) * square)
    return v * half, slope


def adjacency_kernel(
    odd_ref, count_ref, rows_hbm, cols_hbm, tiles_hbm, own_hbm, adj_ref, near_ref,
    rows_ref, cols_ref, tiles_ref, own_ref, sems,
):
    pairs = ((rows_hbm, rows_ref), (cols_hbm, cols_ref), (tiles_hbm, tiles_ref), (own_hbm, own_ref))
    copies = [pltpu.make_async_copy(src, dst, sems.at[i]) for i, (src, dst) in enumerate(pairs)]
    for copy in copies:
        copy.start()
    adj_ref[...] = jnp.zeros_like(adj_ref)
    odd = odd_ref[0]
    for copy in copies:
        copy.wait()
    live = count_ref[0, 0]
    for slot in range(tiles_ref.shape[1]):

        @pl.when(slot < live)
        def _():
            row = pl.multiple_of(rows_ref[0, slot] * TILE, TILE)
            col = cols_ref[0, slot]
            side = col // 2
            part = jnp.where(odd == 1, 2 - side, side)
            col = pl.multiple_of((col - 2 * side) * TILE, TILE)
            adj_ref[part, pl.ds(row, TILE), pl.ds(col, TILE)] = tiles_ref[0, slot]

    near_ref[...] = dot(adj_ref[1], own_ref[0])


def own_kernel(adj_ref, own_ref, w1_ref, w2_ref, agg2_ref, slope_ref, w1_out, w2_out, *, groups):
    hidden = w2_ref.shape[0]
    depth = hidden // groups
    target = lax.broadcasted_iota(jnp.int32, (hidden, hidden), 0)
    source = lax.broadcasted_iota(jnp.int32, (hidden, hidden), 1)
    order = (source == (target % depth) * groups + target // depth).astype(jnp.bfloat16)
    w1 = dot(w1_ref[...], order, 1, 1).astype(jnp.bfloat16)
    w1_out[...] = w1
    w2_out[...] = dot(order, w2_ref[...]).astype(jnp.bfloat16)
    value, slope = gelu_parts(dot(own_ref[...], w1))
    slope_ref[...] = slope
    agg2_ref[...] = dot(adj_ref[1], value.astype(jnp.bfloat16))


def cross_kernel(adj_ref, cross_ref, w1_ref, near_ref, agg2_ref, slope_ref):
    value, slope = gelu_parts(dot(cross_ref[...], w1_ref[...]))
    slope_ref[...] = slope
    agg2_ref[...] = near_ref[...] + dot(adj_ref[0], value.astype(jnp.bfloat16))


def layers_kernel(
    adj_ref, cross_ref, own_ref, other_ref, cot_ref, agg2_ref, own_slope_ref, cross_slope_ref, w1_ref, w2_ref, out_ref
):
    value, slope = gelu_parts(dot(other_ref[...], w1_ref[...]))
    agg2 = agg2_ref[...] + dot(adj_ref[2], value.astype(jnp.bfloat16))
    agg2 = agg2.astype(jnp.bfloat16)
    unused, slope2 = gelu_parts(dot(agg2, w2_ref[...]))
    dpre2 = (cot_ref[0].astype(jnp.float32) * slope2).astype(jnp.bfloat16)
    dagg2 = dot(dpre2, w2_ref[...], 1, 1).astype(jnp.bfloat16)
    first = None
    parts = ((cross_ref, cross_slope_ref[...]), (own_ref, own_slope_ref[...]), (other_ref, slope))
    for part, (ref, slope) in enumerate(parts):
        spread = dot(adj_ref[part], dagg2, 0, 0)
        dpre1 = (spread * slope).astype(jnp.bfloat16)
        term = dot(ref[...], dpre1, 0, 0)
        first = term if first is None else first + term
    second = dot(agg2, dpre2, 0, 0)
    groups, depth = out_ref.shape[0], out_ref.shape[1]
    features = first.shape[0]
    out_ref[:, :, :features] = first.T.astype(jnp.bfloat16).reshape(groups, depth, features)
    out_ref[:, :, features:] = second.astype(jnp.bfloat16).reshape(groups, depth, second.shape[1])


def depth_sum_kernel(in_ref, first_ref, second_ref):
    total = jnp.sum(in_ref[...], axis=0)
    pieces = first_ref.shape[1] // 128
    for piece in range(total.shape[0]):
        ref, place = (first_ref, piece) if piece < pieces else (second_ref, piece - pieces)
        ref[:, place * 128 : (place + 1) * 128] = total[piece : piece + 1, :]


def cross_swap(block):
    count = lax.axis_size(SECTION)
    pairs = [(i, i + 1) for i in range(1, count - 1, 2)]
    return lax.ppermute(block, SECTION, pairs + [(j, i) for i, j in pairs])


def core_swap(block):
    return lax.ppermute(block, "c", [(0, 1), (1, 0)])


def body(features, grad_out, w_first, w_second, tile_values, tile_rows, tile_cols, tile_count):
    own = features[0]
    nodes, in_features = own.shape
    hidden = w_second.shape[0]
    depth = lax.axis_size("z")
    plane = lax.axis_size(PLANE)
    odd = lax.axis_index("c").astype(jnp.int32).reshape(1)

    cross = cross_swap(own)
    other = core_swap(own)
    inputs = (tile_rows, tile_cols, tile_values, features)
    adjacency, near = pl.pallas_call(
        adjacency_kernel,
        out_shape=(
            jax.ShapeDtypeStruct((3, nodes, nodes), jnp.bfloat16),
            jax.ShapeDtypeStruct((nodes, in_features), jnp.float32),
        ),
        in_specs=[SMEM] * 2 + [HBM] * 4,
        out_specs=(VMEM, VMEM),
        scratch_shapes=[pltpu.SMEM(i.shape, i.dtype) for i in inputs[:2]]
        + [pltpu.VMEM(i.shape, i.dtype) for i in inputs[2:]]
        + [pltpu.SemaphoreType.DMA((4,))],
        compiler_params=pltpu.CompilerParams(vmem_limit_bytes=4 * MIB),
        name="adjacency",
    )(odd, tile_count, *[pltpu.with_memory_space_constraint(i, pltpu.HBM) for i in inputs])
    agg1 = near + dot(adjacency[2], other) + dot(adjacency[0], cross)
    agg1 = agg1.astype(jnp.bfloat16)

    cross = cross_swap(agg1)
    other = core_swap(agg1)
    agg2, own_slope, w_first, w_second = pl.pallas_call(
        functools.partial(own_kernel, groups=plane),
        out_shape=(
            jax.ShapeDtypeStruct((nodes, hidden), jnp.float32),
            jax.ShapeDtypeStruct((nodes, hidden), jnp.float32),
            jax.ShapeDtypeStruct(w_first.shape, w_first.dtype),
            jax.ShapeDtypeStruct(w_second.shape, w_second.dtype),
        ),
        in_specs=[VMEM] * 4,
        out_specs=[VMEM] * 4,
        compiler_params=pltpu.CompilerParams(vmem_limit_bytes=12 * MIB),
        cost_estimate=pl.CostEstimate(flops=600_000_000, bytes_accessed=4 * MIB, transcendentals=131072),
        name="own_part",
    )(adjacency, agg1, w_first, w_second)
    agg2, cross_slope = pl.pallas_call(
        cross_kernel,
        out_shape=(
            jax.ShapeDtypeStruct((nodes, hidden), jnp.float32),
            jax.ShapeDtypeStruct((nodes, hidden), jnp.float32),
        ),
        in_specs=[VMEM] * 4,
        out_specs=[VMEM] * 2,
        compiler_params=pltpu.CompilerParams(vmem_limit_bytes=8 * MIB),
        name="cross_part",
    )(adjacency, cross, w_first, agg2)
    gradients = pl.pallas_call(
        layers_kernel,
        out_shape=jax.ShapeDtypeStruct((plane, depth, in_features + hidden), jnp.bfloat16),
        in_specs=[VMEM] * 10,
        out_specs=VMEM,
        compiler_params=pltpu.CompilerParams(vmem_limit_bytes=12 * MIB),
        name="layers",
    )(adjacency, cross, agg1, other, grad_out, agg2, own_slope, cross_slope, w_first, w_second)

    gathered = lax.all_to_all(gradients, PLANE, 0, 0, tiled=True)
    partial = jnp.sum(gathered.astype(jnp.float32), axis=0)
    partial = partial.reshape(depth, (in_features + hidden) // 128, 128)
    collected = lax.all_to_all(partial, "z", 0, 0, tiled=True)
    return pl.pallas_call(
        depth_sum_kernel,
        out_shape=(
            jax.ShapeDtypeStruct((1, in_features), jnp.float32),
            jax.ShapeDtypeStruct((1, hidden), jnp.float32),
        ),
        in_specs=[VMEM],
        out_specs=(VMEM, VMEM),
        compiler_params=pltpu.CompilerParams(vmem_limit_bytes=4 * MIB),
        name="depth_sum",
    )(collected)


def solution(mesh):
    fine = Mesh(mesh.devices.reshape(16, 4, 2, 4), ("z", "y", "c", "x"))
    placed = (
        P("x", SECTION, None),
        P("x", SECTION, None),
        P(),
        P(),
        P("x", SECTION, None, None),
        P("x", SECTION),
        P("x", SECTION),
        P("x", SECTION),
    )
    rows = ("z", "y", "c", "x")
    return jax.shard_map(
        body,
        mesh=fine,
        in_specs=placed,
        out_specs=(P(rows, None), P(rows, None)),
        check_vma=False,
    )
```

```python
import functools

import jax
import jax.numpy as jnp
from jax import lax
from jax.experimental import pallas as pl
from jax.experimental.pallas import tpu as pltpu
from jax.sharding import Mesh
from jax.sharding import PartitionSpec as P

TILE = 128
SECTION = ("z", "y", "c")
PLANE = ("y", "c", "x")
SCALE = 0.7978845608028654
CUBIC = 0.044715
MIB = 1024 * 1024
VMEM = pl.BlockSpec(memory_space=pltpu.VMEM)
HBM = pl.BlockSpec(memory_space=pltpu.HBM)
SMEM = pl.BlockSpec(memory_space=pltpu.SMEM)


def dot(lhs, rhs, lhs_dim=1, rhs_dim=0):
    return lax.dot_general(
        lhs, rhs, (((lhs_dim,), (rhs_dim,)), ((), ())), preferred_element_type=jnp.float32
    )


def gelu_parts(v):
    square = v * v
    t = jnp.tanh(v * (SCALE + (SCALE * CUBIC) * square))
    half = 0.5 + 0.5 * t
    slope = half + (0.5 * v) * (1.0 - t * t) * (SCALE + (3.0 * SCALE * CUBIC) * square)
    return v * half, slope


def adjacency_kernel(
    odd_ref, count_ref, rows_hbm, cols_hbm, tiles_hbm, own_hbm, adj_ref, near_ref,
    rows_ref, cols_ref, tiles_ref, own_ref, sems,
):
    pairs = ((rows_hbm, rows_ref), (cols_hbm, cols_ref), (tiles_hbm, tiles_ref), (own_hbm, own_ref))
    copies = [pltpu.make_async_copy(src, dst, sems.at[i]) for i, (src, dst) in enumerate(pairs)]
    for copy in copies:
        copy.start()
    adj_ref[...] = jnp.zeros_like(adj_ref)
    odd = odd_ref[0]
    for copy in copies:
        copy.wait()
    live = count_ref[0, 0]
    for slot in range(tiles_ref.shape[1]):

        @pl.when(slot < live)
        def _():
            row = pl.multiple_of(rows_ref[0, slot] * TILE, TILE)
            col = cols_ref[0, slot]
            side = col // 2
            part = jnp.where(odd == 1, 2 - side, side)
            col = pl.multiple_of((col - 2 * side) * TILE, TILE)
            adj_ref[part, pl.ds(row, TILE), pl.ds(col, TILE)] = tiles_ref[0, slot]

    near_ref[...] = dot(adj_ref[1], own_ref[0])


def aggregate_kernel(other_ref, adj_ref, near_ref, cross_ref, agg1_ref, sent_ref):
    nodes = agg1_ref.shape[0]
    agg1 = near_ref[...] + dot(adj_ref[2], other_ref[...]) + dot(adj_ref[0], cross_ref[...])
    agg1 = agg1.astype(jnp.bfloat16)
    agg1_ref[...] = agg1
    sent_ref[:nodes, :] = agg1
    sent_ref[nodes:, :] = jnp.zeros((sent_ref.shape[0] - nodes, agg1.shape[1]), agg1.dtype)


def own_kernel(
    adj_ref, own_ref, w1_ref, w2_ref, cot_hbm, agg2_ref, slope_ref, turned_ref, w1_out, w2_out, cot_ref, sem, *, groups
):
    copy = pltpu.make_async_copy(cot_hbm.at[0], cot_ref, sem)
    copy.start()
    hidden = w2_ref.shape[0]
    depth = hidden // groups
    target = lax.broadcasted_iota(jnp.int32, (hidden, hidden), 0)
    source = lax.broadcasted_iota(jnp.int32, (hidden, hidden), 1)
    order = (source == (target % depth) * groups + target // depth).astype(jnp.bfloat16)
    w1 = dot(w1_ref[...], order, 1, 1).astype(jnp.bfloat16)
    w1_out[...] = w1
    w2_out[...] = dot(order, w2_ref[...]).astype(jnp.bfloat16)
    value, slope = gelu_parts(dot(own_ref[...], w1))
    slope_ref[...] = slope
    agg2_ref[...] = dot(adj_ref[1], value.astype(jnp.bfloat16))
    nodes = own_ref.shape[0]
    for part in range(3):
        turned_ref[part * nodes : (part + 1) * nodes, :] = adj_ref[part].T
    copy.wait()


def other_kernel(adj_ref, other_ref, w1_ref, near_ref, agg2_ref, slope_ref):
    value, slope = gelu_parts(dot(other_ref[...], w1_ref[...]))
    slope_ref[...] = slope
    agg2_ref[...] = near_ref[...] + dot(adj_ref[2], value.astype(jnp.bfloat16))


def layers_kernel(
    adj_ref, cross_ref, own_ref, other_ref, cot_ref, agg2_ref, own_slope_ref, other_slope_ref, turned_ref,
    w1_ref, w2_ref, out_ref,
):
    nodes, features = own_ref.shape
    cross = cross_ref[:nodes, :]
    value, slope = gelu_parts(dot(cross, w1_ref[...]))
    agg2 = agg2_ref[...] + dot(adj_ref[0], value.astype(jnp.bfloat16))
    agg2 = agg2.astype(jnp.bfloat16)
    unused, slope2 = gelu_parts(dot(agg2, w2_ref[...]))
    dpre2 = (cot_ref[...].astype(jnp.float32) * slope2).astype(jnp.bfloat16)
    dagg2 = dot(dpre2, w2_ref[...], 1, 1).astype(jnp.bfloat16)
    groups, depth = out_ref.shape[0], out_ref.shape[1]
    second = dot(agg2.T, dpre2)
    out_ref[:, :, features:] = second.astype(jnp.bfloat16).reshape(groups, depth, second.shape[1])
    spread = dot(turned_ref[...], dagg2)
    slopes = (slope, own_slope_ref[...], other_slope_ref[...])
    dpre1 = [
        (spread[part * nodes : (part + 1) * nodes] * slope).astype(jnp.bfloat16)
        for part, slope in enumerate(slopes)
    ]
    agg1 = jnp.concatenate([cross, own_ref[...], other_ref[...]], axis=0)
    first = dot(agg1.T, jnp.concatenate(dpre1, axis=0)).astype(jnp.bfloat16).T
    out_ref[:, :, :features] = first.reshape(groups, depth, features)


def depth_sum_kernel(in_ref, first_ref, second_ref):
    total = jnp.sum(in_ref[...], axis=0)
    pieces = first_ref.shape[1] // 128
    for piece in range(total.shape[0]):
        ref, place = (first_ref, piece) if piece < pieces else (second_ref, piece - pieces)
        ref[:, place * 128 : (place + 1) * 128] = total[piece : piece + 1, :]


def cross_swap(block):
    count = lax.axis_size(SECTION)
    pairs = [(i, i + 1) for i in range(1, count - 1, 2)]
    return lax.ppermute(block, SECTION, pairs + [(j, i) for i, j in pairs])


def core_swap(block):
    return lax.ppermute(block, "c", [(0, 1), (1, 0)])


def body(features, grad_out, w_first, w_second, tile_values, tile_rows, tile_cols, tile_count):
    own = features[0]
    nodes, in_features = own.shape
    hidden = w_second.shape[0]
    depth = lax.axis_size("z")
    plane = lax.axis_size(PLANE)
    odd = lax.axis_index("c").astype(jnp.int32).reshape(1)

    cross = cross_swap(own)
    other = core_swap(own)
    inputs = (tile_rows, tile_cols, tile_values, features)
    adjacency, near = pl.pallas_call(
        adjacency_kernel,
        out_shape=(
            jax.ShapeDtypeStruct((3, nodes, nodes), jnp.bfloat16),
            jax.ShapeDtypeStruct((nodes, in_features), jnp.float32),
        ),
        in_specs=[SMEM] * 2 + [HBM] * 4,
        out_specs=(VMEM, VMEM),
        scratch_shapes=[pltpu.SMEM(i.shape, i.dtype) for i in inputs[:2]]
        + [pltpu.VMEM(i.shape, i.dtype) for i in inputs[2:]]
        + [pltpu.SemaphoreType.DMA((4,))],
        compiler_params=pltpu.CompilerParams(vmem_limit_bytes=4 * MIB),
        name="adjacency",
    )(odd, tile_count, *[pltpu.with_memory_space_constraint(i, pltpu.HBM) for i in inputs])
    agg1, sent = pl.pallas_call(
        aggregate_kernel,
        out_shape=(
            jax.ShapeDtypeStruct((nodes, in_features), jnp.bfloat16),
            jax.ShapeDtypeStruct((nodes + 16, in_features), jnp.bfloat16),
        ),
        in_specs=[VMEM] * 4,
        out_specs=(VMEM, VMEM),
        compiler_params=pltpu.CompilerParams(vmem_limit_bytes=4 * MIB),
        name="aggregate",
    )(other, adjacency, near, cross)

    cross = cross_swap(sent)
    other = core_swap(agg1)
    agg2, own_slope, turned, w_first, w_second, cotangent = pl.pallas_call(
        functools.partial(own_kernel, groups=plane),
        out_shape=(
            jax.ShapeDtypeStruct((nodes, hidden), jnp.float32),
            jax.ShapeDtypeStruct((nodes, hidden), jnp.float32),
            jax.ShapeDtypeStruct((3 * nodes, nodes), jnp.bfloat16),
            jax.ShapeDtypeStruct(w_first.shape, w_first.dtype),
            jax.ShapeDtypeStruct(w_second.shape, w_second.dtype),
            jax.ShapeDtypeStruct((nodes, hidden), grad_out.dtype),
        ),
        in_specs=[VMEM] * 4 + [HBM],
        out_specs=[VMEM] * 6,
        scratch_shapes=[pltpu.SemaphoreType.DMA],
        compiler_params=pltpu.CompilerParams(vmem_limit_bytes=12 * MIB),
        cost_estimate=pl.CostEstimate(flops=600_000_000, bytes_accessed=4 * MIB, transcendentals=131072),
        name="own_part",
    )(adjacency, agg1, w_first, w_second, pltpu.with_memory_space_constraint(grad_out, pltpu.HBM))
    agg2, other_slope = pl.pallas_call(
        other_kernel,
        out_shape=(
            jax.ShapeDtypeStruct((nodes, hidden), jnp.float32),
            jax.ShapeDtypeStruct((nodes, hidden), jnp.float32),
        ),
        in_specs=[VMEM] * 4,
        out_specs=[VMEM] * 2,
        compiler_params=pltpu.CompilerParams(vmem_limit_bytes=8 * MIB),
        name="other_part",
    )(adjacency, other, w_first, agg2)
    gradients = pl.pallas_call(
        layers_kernel,
        out_shape=jax.ShapeDtypeStruct((plane, depth, in_features + hidden), jnp.bfloat16),
        in_specs=[VMEM] * 11,
        out_specs=VMEM,
        compiler_params=pltpu.CompilerParams(vmem_limit_bytes=12 * MIB),
        name="layers",
    )(adjacency, cross, agg1, other, cotangent, agg2, own_slope, other_slope, turned, w_first, w_second)

    gathered = lax.all_to_all(gradients, PLANE, 0, 0, tiled=True)
    partial = jnp.sum(gathered.astype(jnp.float32), axis=0)
    partial = partial.reshape(depth, (in_features + hidden) // 128, 128)
    collected = lax.all_to_all(partial, "z", 0, 0, tiled=True)
    return pl.pallas_call(
        depth_sum_kernel,
        out_shape=(
            jax.ShapeDtypeStruct((1, in_features), jnp.float32),
            jax.ShapeDtypeStruct((1, hidden), jnp.float32),
        ),
        in_specs=[VMEM],
        out_specs=(VMEM, VMEM),
        compiler_params=pltpu.CompilerParams(vmem_limit_bytes=4 * MIB),
        name="depth_sum",
    )(collected)


def solution(mesh):
    fine = Mesh(mesh.devices.reshape(16, 4, 2, 4), ("z", "y", "c", "x"))
    placed = (
        P("x", SECTION, None),
        P("x", SECTION, None),
        P(),
        P(),
        P("x", SECTION, None, None),
        P("x", SECTION),
        P("x", SECTION),
        P("x", SECTION),
    )
    rows = ("z", "y", "c", "x")
    return jax.shard_map(
        body,
        mesh=fine,
        in_specs=placed,
        out_specs=(P(rows, None), P(rows, None)),
        check_vma=False,
    )
```

```python
import functools

import jax
import jax.numpy as jnp
from jax import lax
from jax.experimental import pallas as pl
from jax.experimental.pallas import tpu as pltpu
from jax.sharding import Mesh
from jax.sharding import PartitionSpec as P

TILE = 128
SECTION = ("z", "y", "c")
PLANE = ("y", "c", "x")
SCALE = 0.7978845608028654
CUBIC = 0.044715
MIB = 1024 * 1024
DEPTH_FIRST = 8
PLANE_FIRST = 30
VMEM = pl.BlockSpec(memory_space=pltpu.VMEM)
HBM = pl.BlockSpec(memory_space=pltpu.HBM)
SMEM = pl.BlockSpec(memory_space=pltpu.SMEM)


def dot(lhs, rhs, lhs_dim=1, rhs_dim=0):
    return lax.dot_general(
        lhs, rhs, (((lhs_dim,), (rhs_dim,)), ((), ())), preferred_element_type=jnp.float32
    )


def gelu_parts(v):
    square = v * v
    t = jnp.tanh(v * (SCALE + (SCALE * CUBIC) * square))
    half = 0.5 + 0.5 * t
    slope = half + (0.5 * v) * (1.0 - t * t) * (SCALE + (3.0 * SCALE * CUBIC) * square)
    return v * half, slope


def adjacency_kernel(
    odd_ref, count_ref, rows_hbm, cols_hbm, tiles_hbm, own_hbm, adj_ref, near_ref,
    rows_ref, cols_ref, tiles_ref, own_ref, sems,
):
    pairs = ((rows_hbm, rows_ref), (cols_hbm, cols_ref), (tiles_hbm, tiles_ref), (own_hbm, own_ref))
    copies = [pltpu.make_async_copy(src, dst, sems.at[i]) for i, (src, dst) in enumerate(pairs)]
    for copy in copies:
        copy.start()
    adj_ref[...] = jnp.zeros_like(adj_ref)
    odd = odd_ref[0]
    for copy in copies:
        copy.wait()
    live = count_ref[0, 0]
    for slot in range(tiles_ref.shape[1]):

        @pl.when(slot < live)
        def _():
            row = pl.multiple_of(rows_ref[0, slot] * TILE, TILE)
            col = cols_ref[0, slot]
            side = col // 2
            part = jnp.where(odd == 1, 2 - side, side)
            col = pl.multiple_of((col - 2 * side) * TILE, TILE)
            adj_ref[part, pl.ds(row, TILE), pl.ds(col, TILE)] = tiles_ref[0, slot]

    near_ref[...] = dot(adj_ref[1], own_ref[0])


def aggregate_kernel(other_ref, adj_ref, near_ref, cross_ref, agg1_ref, sent_ref):
    nodes = agg1_ref.shape[0]
    agg1 = near_ref[...] + dot(adj_ref[2], other_ref[...]) + dot(adj_ref[0], cross_ref[...])
    agg1 = agg1.astype(jnp.bfloat16)
    agg1_ref[...] = agg1
    sent_ref[:nodes, :] = agg1
    sent_ref[nodes:, :] = jnp.zeros((sent_ref.shape[0] - nodes, agg1.shape[1]), agg1.dtype)


def own_kernel(
    adj_ref, own_ref, w1_ref, w2_ref, cot_hbm, agg2_ref, slope_ref, turned_ref, w1_out, w2_out, cot_ref, sem, *, groups
):
    copy = pltpu.make_async_copy(cot_hbm.at[0], cot_ref, sem)
    copy.start()
    hidden = w2_ref.shape[0]
    depth = hidden // groups
    target = lax.broadcasted_iota(jnp.int32, (hidden, hidden), 0)
    source = lax.broadcasted_iota(jnp.int32, (hidden, hidden), 1)
    plane = (target % depth + DEPTH_FIRST) % depth
    place = (target // depth + PLANE_FIRST) % groups
    order = (source == plane * groups + place).astype(jnp.bfloat16)
    w1 = dot(w1_ref[...], order, 1, 1).astype(jnp.bfloat16)
    w1_out[...] = w1
    w2_out[...] = dot(order, w2_ref[...]).astype(jnp.bfloat16)
    value, slope = gelu_parts(dot(own_ref[...], w1))
    slope_ref[...] = slope
    agg2_ref[...] = dot(adj_ref[1], value.astype(jnp.bfloat16))
    nodes = own_ref.shape[0]
    for part in range(3):
        turned_ref[part * nodes : (part + 1) * nodes, :] = adj_ref[part].T
    copy.wait()


def other_kernel(adj_ref, other_ref, w1_ref, near_ref, agg2_ref, slope_ref):
    value, slope = gelu_parts(dot(other_ref[...], w1_ref[...]))
    slope_ref[...] = slope
    agg2_ref[...] = near_ref[...] + dot(adj_ref[2], value.astype(jnp.bfloat16))


def layers_kernel(
    adj_ref, cross_ref, own_ref, other_ref, cot_ref, agg2_ref, own_slope_ref, other_slope_ref, turned_ref,
    w1_ref, w2_ref, out_ref,
):
    nodes, features = own_ref.shape
    cross = cross_ref[:nodes, :]
    value, slope = gelu_parts(dot(cross, w1_ref[...]))
    agg2 = agg2_ref[...] + dot(adj_ref[0], value.astype(jnp.bfloat16))
    agg2 = agg2.astype(jnp.bfloat16)
    unused, slope2 = gelu_parts(dot(agg2, w2_ref[...]))
    dpre2 = (cot_ref[...].astype(jnp.float32) * slope2).astype(jnp.bfloat16)
    dagg2 = dot(dpre2, w2_ref[...], 1, 1).astype(jnp.bfloat16)
    groups, depth = out_ref.shape[0], out_ref.shape[1]
    second = dot(agg2.T, dpre2)
    out_ref[:, :, features:] = second.astype(jnp.bfloat16).reshape(groups, depth, second.shape[1])
    spread = dot(turned_ref[...], dagg2)
    slopes = (slope, own_slope_ref[...], other_slope_ref[...])
    dpre1 = [
        (spread[part * nodes : (part + 1) * nodes] * slope).astype(jnp.bfloat16)
        for part, slope in enumerate(slopes)
    ]
    agg1 = jnp.concatenate([cross, own_ref[...], other_ref[...]], axis=0)
    first = dot(agg1.T, jnp.concatenate(dpre1, axis=0)).astype(jnp.bfloat16).T
    out_ref[:, :, :features] = first.reshape(groups, depth, features)


def depth_sum_kernel(in_ref, first_ref, second_ref):
    total = jnp.sum(in_ref[...].astype(jnp.float32), axis=0)
    pieces = first_ref.shape[1] // 128
    for piece in range(total.shape[0]):
        ref, place = (first_ref, piece) if piece < pieces else (second_ref, piece - pieces)
        ref[:, place * 128 : (place + 1) * 128] = total[piece : piece + 1, :]


def cross_swap(block):
    count = lax.axis_size(SECTION)
    pairs = [(i, i + 1) for i in range(1, count - 1, 2)]
    return lax.ppermute(block, SECTION, pairs + [(j, i) for i, j in pairs])


def core_swap(block):
    return lax.ppermute(block, "c", [(0, 1), (1, 0)])


def body(features, grad_out, w_first, w_second, tile_values, tile_rows, tile_cols, tile_count):
    own = features[0]
    nodes, in_features = own.shape
    hidden = w_second.shape[0]
    depth = lax.axis_size("z")
    plane = lax.axis_size(PLANE)
    odd = lax.axis_index("c").astype(jnp.int32).reshape(1)

    cross = cross_swap(own)
    other = core_swap(own)
    inputs = (tile_rows, tile_cols, tile_values, features)
    adjacency, near = pl.pallas_call(
        adjacency_kernel,
        out_shape=(
            jax.ShapeDtypeStruct((3, nodes, nodes), jnp.bfloat16),
            jax.ShapeDtypeStruct((nodes, in_features), jnp.float32),
        ),
        in_specs=[SMEM] * 2 + [HBM] * 4,
        out_specs=(VMEM, VMEM),
        scratch_shapes=[pltpu.SMEM(i.shape, i.dtype) for i in inputs[:2]]
        + [pltpu.VMEM(i.shape, i.dtype) for i in inputs[2:]]
        + [pltpu.SemaphoreType.DMA((4,))],
        compiler_params=pltpu.CompilerParams(vmem_limit_bytes=4 * MIB),
        name="adjacency",
    )(odd, tile_count, *[pltpu.with_memory_space_constraint(i, pltpu.HBM) for i in inputs])
    agg1, sent = pl.pallas_call(
        aggregate_kernel,
        out_shape=(
            jax.ShapeDtypeStruct((nodes, in_features), jnp.bfloat16),
            jax.ShapeDtypeStruct((nodes + 16, in_features), jnp.bfloat16),
        ),
        in_specs=[VMEM] * 4,
        out_specs=(VMEM, VMEM),
        compiler_params=pltpu.CompilerParams(vmem_limit_bytes=4 * MIB),
        name="aggregate",
    )(other, adjacency, near, cross)

    cross = cross_swap(sent)
    other = core_swap(agg1)
    agg2, own_slope, turned, w_first, w_second, cotangent = pl.pallas_call(
        functools.partial(own_kernel, groups=plane),
        out_shape=(
            jax.ShapeDtypeStruct((nodes, hidden), jnp.float32),
            jax.ShapeDtypeStruct((nodes, hidden), jnp.float32),
            jax.ShapeDtypeStruct((3 * nodes, nodes), jnp.bfloat16),
            jax.ShapeDtypeStruct(w_first.shape, w_first.dtype),
            jax.ShapeDtypeStruct(w_second.shape, w_second.dtype),
            jax.ShapeDtypeStruct((nodes, hidden), grad_out.dtype),
        ),
        in_specs=[VMEM] * 4 + [HBM],
        out_specs=[VMEM] * 6,
        scratch_shapes=[pltpu.SemaphoreType.DMA],
        compiler_params=pltpu.CompilerParams(vmem_limit_bytes=12 * MIB),
        cost_estimate=pl.CostEstimate(flops=600_000_000, bytes_accessed=4 * MIB, transcendentals=131072),
        name="own_part",
    )(adjacency, agg1, w_first, w_second, pltpu.with_memory_space_constraint(grad_out, pltpu.HBM))
    agg2, other_slope = pl.pallas_call(
        other_kernel,
        out_shape=(
            jax.ShapeDtypeStruct((nodes, hidden), jnp.float32),
            jax.ShapeDtypeStruct((nodes, hidden), jnp.float32),
        ),
        in_specs=[VMEM] * 4,
        out_specs=[VMEM] * 2,
        compiler_params=pltpu.CompilerParams(vmem_limit_bytes=8 * MIB),
        name="other_part",
    )(adjacency, other, w_first, agg2)
    gradients = pl.pallas_call(
        layers_kernel,
        out_shape=jax.ShapeDtypeStruct((plane, depth, in_features + hidden), jnp.bfloat16),
        in_specs=[VMEM] * 11,
        out_specs=VMEM,
        compiler_params=pltpu.CompilerParams(vmem_limit_bytes=12 * MIB),
        name="layers",
    )(adjacency, cross, agg1, other, cotangent, agg2, own_slope, other_slope, turned, w_first, w_second)

    groups = [[(i + PLANE_FIRST) % plane for i in range(plane)]]
    gathered = lax.all_to_all(gradients, PLANE, 0, 0, axis_index_groups=groups, tiled=True)
    partial = jnp.sum(gathered.astype(jnp.float32), axis=0)
    partial = partial.astype(jnp.bfloat16).reshape(depth, (in_features + hidden) // 128, 128)
    groups = [[(i + DEPTH_FIRST) % depth for i in range(depth)]]
    collected = lax.all_to_all(partial, "z", 0, 0, axis_index_groups=groups, tiled=True)
    return pl.pallas_call(
        depth_sum_kernel,
        out_shape=(
            jax.ShapeDtypeStruct((1, in_features), jnp.float32),
            jax.ShapeDtypeStruct((1, hidden), jnp.float32),
        ),
        in_specs=[VMEM],
        out_specs=(VMEM, VMEM),
        compiler_params=pltpu.CompilerParams(vmem_limit_bytes=4 * MIB),
        name="depth_sum",
    )(collected)


def solution(mesh):
    fine = Mesh(mesh.devices.reshape(16, 4, 2, 4), ("z", "y", "c", "x"))
    placed = (
        P("x", SECTION, None),
        P("x", SECTION, None),
        P(),
        P(),
        P("x", SECTION, None, None),
        P("x", SECTION),
        P("x", SECTION),
        P("x", SECTION),
    )
    rows = ("z", "y", "c", "x")
    return jax.shard_map(
        body,
        mesh=fine,
        in_specs=placed,
        out_specs=(P(rows, None), P(rows, None)),
        check_vma=False,
    )
```

```python
import functools

import jax
import jax.numpy as jnp
from jax import lax
from jax.experimental import pallas as pl
from jax.experimental.pallas import tpu as pltpu
from jax.sharding import Mesh
from jax.sharding import PartitionSpec as P

TILE = 128
SECTION = ("z", "y", "c")
PLANE = ("y", "c", "x")
SCALE = 0.7978845608028654
CUBIC = 0.044715
MIB = 1024 * 1024
DEPTH_FIRST = 9
PLANE_FIRST = 22
VMEM = pl.BlockSpec(memory_space=pltpu.VMEM)
HBM = pl.BlockSpec(memory_space=pltpu.HBM)
SMEM = pl.BlockSpec(memory_space=pltpu.SMEM)


def dot(lhs, rhs, lhs_dim=1, rhs_dim=0):
    return lax.dot_general(
        lhs, rhs, (((lhs_dim,), (rhs_dim,)), ((), ())), preferred_element_type=jnp.float32
    )


def gelu_parts(v):
    square = v * v
    t = jnp.tanh(v * (SCALE + (SCALE * CUBIC) * square))
    half = 0.5 + 0.5 * t
    slope = half + (0.5 * v) * (1.0 - t * t) * (SCALE + (3.0 * SCALE * CUBIC) * square)
    return v * half, slope


def adjacency_kernel(
    odd_ref, count_ref, rows_hbm, cols_hbm, tiles_hbm, own_hbm, adj_ref, near_ref,
    rows_ref, cols_ref, tiles_ref, own_ref, sems,
):
    pairs = ((rows_hbm, rows_ref), (cols_hbm, cols_ref), (tiles_hbm, tiles_ref), (own_hbm, own_ref))
    copies = [pltpu.make_async_copy(src, dst, sems.at[i]) for i, (src, dst) in enumerate(pairs)]
    for copy in copies:
        copy.start()
    adj_ref[...] = jnp.zeros_like(adj_ref)
    odd = odd_ref[0]
    for copy in copies:
        copy.wait()
    live = count_ref[0, 0]
    for slot in range(tiles_ref.shape[1]):

        @pl.when(slot < live)
        def _():
            row = pl.multiple_of(rows_ref[0, slot] * TILE, TILE)
            col = cols_ref[0, slot]
            side = col // 2
            part = jnp.where(odd == 1, 2 - side, side)
            col = pl.multiple_of((col - 2 * side) * TILE, TILE)
            adj_ref[part, pl.ds(row, TILE), pl.ds(col, TILE)] = tiles_ref[0, slot]

    near_ref[...] = dot(adj_ref[1], own_ref[0])


def aggregate_kernel(other_ref, adj_ref, near_ref, cross_ref, agg1_ref, sent_ref):
    nodes = agg1_ref.shape[0]
    agg1 = near_ref[...] + dot(adj_ref[2], other_ref[...]) + dot(adj_ref[0], cross_ref[...])
    agg1 = agg1.astype(jnp.bfloat16)
    agg1_ref[...] = agg1
    sent_ref[:nodes, :] = agg1
    sent_ref[nodes:, :] = jnp.zeros((sent_ref.shape[0] - nodes, agg1.shape[1]), agg1.dtype)


def own_kernel(
    adj_ref, own_ref, w1_ref, w2_ref, cot_hbm, agg2_ref, slope_ref, turned_ref, w1_out, w2_out, cot_ref, sem, *, groups
):
    copy = pltpu.make_async_copy(cot_hbm.at[0], cot_ref, sem)
    copy.start()
    hidden = w2_ref.shape[0]
    depth = hidden // groups
    target = lax.broadcasted_iota(jnp.int32, (hidden, hidden), 0)
    source = lax.broadcasted_iota(jnp.int32, (hidden, hidden), 1)
    plane = (target % depth + DEPTH_FIRST) % depth
    place = (target // depth + PLANE_FIRST) % groups
    order = (source == plane * groups + place).astype(jnp.bfloat16)
    w1 = dot(w1_ref[...], order, 1, 1).astype(jnp.bfloat16)
    w1_out[...] = w1
    w2_out[...] = dot(order, w2_ref[...]).astype(jnp.bfloat16)
    value, slope = gelu_parts(dot(own_ref[...], w1))
    slope_ref[...] = slope
    agg2_ref[...] = dot(adj_ref[1], value.astype(jnp.bfloat16))
    nodes = own_ref.shape[0]
    for part in range(3):
        turned_ref[part * nodes : (part + 1) * nodes, :] = adj_ref[part].T
    copy.wait()


def other_kernel(adj_ref, other_ref, w1_ref, near_ref, agg2_ref, slope_ref):
    value, slope = gelu_parts(dot(other_ref[...], w1_ref[...]))
    slope_ref[...] = slope
    agg2_ref[...] = near_ref[...] + dot(adj_ref[2], value.astype(jnp.bfloat16))


def layers_kernel(
    adj_ref, cross_ref, own_ref, other_ref, cot_ref, agg2_ref, own_slope_ref, other_slope_ref, turned_ref,
    w1_ref, w2_ref, out_ref,
):
    nodes, features = own_ref.shape
    cross = cross_ref[:nodes, :]
    value, slope = gelu_parts(dot(cross, w1_ref[...]))
    agg2 = agg2_ref[...] + dot(adj_ref[0], value.astype(jnp.bfloat16))
    agg2 = agg2.astype(jnp.bfloat16)
    unused, slope2 = gelu_parts(dot(agg2, w2_ref[...]))
    dpre2 = (cot_ref[...].astype(jnp.float32) * slope2).astype(jnp.bfloat16)
    dagg2 = dot(dpre2, w2_ref[...], 1, 1).astype(jnp.bfloat16)
    groups, depth = out_ref.shape[0], out_ref.shape[1]
    second = dot(agg2.T, dpre2)
    out_ref[:, :, features:] = second.astype(jnp.bfloat16).reshape(groups, depth, second.shape[1])
    spread = dot(turned_ref[...], dagg2)
    slopes = (slope, own_slope_ref[...], other_slope_ref[...])
    dpre1 = [
        (spread[part * nodes : (part + 1) * nodes] * slope).astype(jnp.bfloat16)
        for part, slope in enumerate(slopes)
    ]
    agg1 = jnp.concatenate([cross, own_ref[...], other_ref[...]], axis=0)
    first = dot(agg1.T, jnp.concatenate(dpre1, axis=0)).astype(jnp.bfloat16).T
    out_ref[:, :, :features] = first.reshape(groups, depth, features)


def depth_sum_kernel(in_ref, first_ref, second_ref):
    total = jnp.sum(in_ref[...].astype(jnp.float32), axis=0)
    pieces = first_ref.shape[1] // 128
    for piece in range(total.shape[0]):
        ref, place = (first_ref, piece) if piece < pieces else (second_ref, piece - pieces)
        ref[:, place * 128 : (place + 1) * 128] = total[piece : piece + 1, :]


def cross_swap(block):
    count = lax.axis_size(SECTION)
    pairs = [(i, i + 1) for i in range(1, count - 1, 2)]
    return lax.ppermute(block, SECTION, pairs + [(j, i) for i, j in pairs])


def core_swap(block):
    return lax.ppermute(block, "c", [(0, 1), (1, 0)])


def body(features, grad_out, w_first, w_second, tile_values, tile_rows, tile_cols, tile_count):
    own = features[0]
    nodes, in_features = own.shape
    hidden = w_second.shape[0]
    depth = lax.axis_size("z")
    plane = lax.axis_size(PLANE)
    odd = lax.axis_index("c").astype(jnp.int32).reshape(1)

    cross = cross_swap(own)
    other = core_swap(own)
    inputs = (tile_rows, tile_cols, tile_values, features)
    adjacency, near = pl.pallas_call(
        adjacency_kernel,
        out_shape=(
            jax.ShapeDtypeStruct((3, nodes, nodes), jnp.bfloat16),
            jax.ShapeDtypeStruct((nodes, in_features), jnp.float32),
        ),
        in_specs=[SMEM] * 2 + [HBM] * 4,
        out_specs=(VMEM, VMEM),
        scratch_shapes=[pltpu.SMEM(i.shape, i.dtype) for i in inputs[:2]]
        + [pltpu.VMEM(i.shape, i.dtype) for i in inputs[2:]]
        + [pltpu.SemaphoreType.DMA((4,))],
        compiler_params=pltpu.CompilerParams(vmem_limit_bytes=4 * MIB),
        name="adjacency",
    )(odd, tile_count, *[pltpu.with_memory_space_constraint(i, pltpu.HBM) for i in inputs])
    agg1, sent = pl.pallas_call(
        aggregate_kernel,
        out_shape=(
            jax.ShapeDtypeStruct((nodes, in_features), jnp.bfloat16),
            jax.ShapeDtypeStruct((nodes + 16, in_features), jnp.bfloat16),
        ),
        in_specs=[VMEM] * 4,
        out_specs=(VMEM, VMEM),
        compiler_params=pltpu.CompilerParams(vmem_limit_bytes=4 * MIB),
        name="aggregate",
    )(other, adjacency, near, cross)

    cross = cross_swap(sent)
    other = core_swap(agg1)
    agg2, own_slope, turned, w_first, w_second, cotangent = pl.pallas_call(
        functools.partial(own_kernel, groups=plane),
        out_shape=(
            jax.ShapeDtypeStruct((nodes, hidden), jnp.float32),
            jax.ShapeDtypeStruct((nodes, hidden), jnp.float32),
            jax.ShapeDtypeStruct((3 * nodes, nodes), jnp.bfloat16),
            jax.ShapeDtypeStruct(w_first.shape, w_first.dtype),
            jax.ShapeDtypeStruct(w_second.shape, w_second.dtype),
            jax.ShapeDtypeStruct((nodes, hidden), grad_out.dtype),
        ),
        in_specs=[VMEM] * 4 + [HBM],
        out_specs=[VMEM] * 6,
        scratch_shapes=[pltpu.SemaphoreType.DMA],
        compiler_params=pltpu.CompilerParams(vmem_limit_bytes=12 * MIB),
        cost_estimate=pl.CostEstimate(flops=600_000_000, bytes_accessed=4 * MIB, transcendentals=131072),
        name="own_part",
    )(adjacency, agg1, w_first, w_second, pltpu.with_memory_space_constraint(grad_out, pltpu.HBM))
    agg2, other_slope = pl.pallas_call(
        other_kernel,
        out_shape=(
            jax.ShapeDtypeStruct((nodes, hidden), jnp.float32),
            jax.ShapeDtypeStruct((nodes, hidden), jnp.float32),
        ),
        in_specs=[VMEM] * 4,
        out_specs=[VMEM] * 2,
        compiler_params=pltpu.CompilerParams(vmem_limit_bytes=8 * MIB),
        name="other_part",
    )(adjacency, other, w_first, agg2)
    gradients = pl.pallas_call(
        layers_kernel,
        out_shape=jax.ShapeDtypeStruct((plane, depth, in_features + hidden), jnp.bfloat16),
        in_specs=[VMEM] * 11,
        out_specs=VMEM,
        compiler_params=pltpu.CompilerParams(vmem_limit_bytes=12 * MIB),
        name="layers",
    )(adjacency, cross, agg1, other, cotangent, agg2, own_slope, other_slope, turned, w_first, w_second)

    groups = [[(i + PLANE_FIRST) % plane for i in range(plane)]]
    gathered = lax.all_to_all(gradients, PLANE, 0, 0, axis_index_groups=groups, tiled=True)
    partial = jnp.sum(gathered.astype(jnp.float32), axis=0)
    partial = partial.astype(jnp.bfloat16).reshape(depth, (in_features + hidden) // 128, 128)
    groups = [[(i + DEPTH_FIRST) % depth for i in range(depth)]]
    collected = lax.all_to_all(partial, "z", 0, 0, axis_index_groups=groups, tiled=True)
    return pl.pallas_call(
        depth_sum_kernel,
        out_shape=(
            jax.ShapeDtypeStruct((1, in_features), jnp.float32),
            jax.ShapeDtypeStruct((1, hidden), jnp.float32),
        ),
        in_specs=[VMEM],
        out_specs=(VMEM, VMEM),
        compiler_params=pltpu.CompilerParams(vmem_limit_bytes=4 * MIB),
        name="depth_sum",
    )(collected)


def solution(mesh):
    fine = Mesh(mesh.devices.reshape(16, 4, 2, 4), ("z", "y", "c", "x"))
    placed = (
        P("x", SECTION, None),
        P("x", SECTION, None),
        P(),
        P(),
        P("x", SECTION, None, None),
        P("x", SECTION),
        P("x", SECTION),
        P("x", SECTION),
    )
    rows = ("z", "y", "c", "x")
    return jax.shard_map(
        body,
        mesh=fine,
        in_specs=placed,
        out_specs=(P(rows, None), P(rows, None)),
        check_vma=False,
    )
```

```python
import functools

import jax
import jax.numpy as jnp
from jax import lax
from jax.experimental import pallas as pl
from jax.experimental.pallas import tpu as pltpu
from jax.sharding import Mesh
from jax.sharding import PartitionSpec as P

TILE = 128
SECTION = ("z", "y", "c")
PLANE = ("y", "c", "x")
SCALE = 0.7978845608028654
CUBIC = 0.044715
MIB = 1024 * 1024
DEPTH_FIRST = 10
PLANE_FIRST = 22
VMEM = pl.BlockSpec(memory_space=pltpu.VMEM)
HBM = pl.BlockSpec(memory_space=pltpu.HBM)
SMEM = pl.BlockSpec(memory_space=pltpu.SMEM)


def dot(lhs, rhs, lhs_dim=1, rhs_dim=0):
    return lax.dot_general(
        lhs, rhs, (((lhs_dim,), (rhs_dim,)), ((), ())), preferred_element_type=jnp.float32
    )


def gelu_parts(v):
    square = v * v
    t = jnp.tanh(v * (SCALE + (SCALE * CUBIC) * square))
    half = 0.5 + 0.5 * t
    slope = half + (0.5 * v) * (1.0 - t * t) * (SCALE + (3.0 * SCALE * CUBIC) * square)
    return v * half, slope


def adjacency_kernel(
    odd_ref, count_ref, rows_hbm, cols_hbm, tiles_hbm, own_hbm, adj_ref, near_ref,
    rows_ref, cols_ref, tiles_ref, own_ref, sems,
):
    pairs = ((rows_hbm, rows_ref), (cols_hbm, cols_ref), (tiles_hbm, tiles_ref), (own_hbm, own_ref))
    copies = [pltpu.make_async_copy(src, dst, sems.at[i]) for i, (src, dst) in enumerate(pairs)]
    for copy in copies:
        copy.start()
    adj_ref[...] = jnp.zeros_like(adj_ref)
    odd = odd_ref[0]
    for copy in copies:
        copy.wait()
    live = count_ref[0, 0]
    for slot in range(tiles_ref.shape[1]):

        @pl.when(slot < live)
        def _():
            row = pl.multiple_of(rows_ref[0, slot] * TILE, TILE)
            col = cols_ref[0, slot]
            side = col // 2
            part = jnp.where(odd == 1, 2 - side, side)
            col = pl.multiple_of((col - 2 * side) * TILE, TILE)
            adj_ref[part, pl.ds(row, TILE), pl.ds(col, TILE)] = tiles_ref[0, slot]

    near_ref[...] = dot(adj_ref[1], own_ref[0])


def aggregate_kernel(other_ref, adj_ref, near_ref, cross_ref, agg1_ref, sent_ref):
    nodes = agg1_ref.shape[0]
    agg1 = near_ref[...] + dot(adj_ref[2], other_ref[...]) + dot(adj_ref[0], cross_ref[...])
    agg1 = agg1.astype(jnp.bfloat16)
    agg1_ref[...] = agg1
    sent_ref[:nodes, :] = agg1
    sent_ref[nodes:, :] = jnp.zeros((sent_ref.shape[0] - nodes, agg1.shape[1]), agg1.dtype)


def own_kernel(
    adj_ref, own_ref, w1_ref, w2_ref, cot_hbm, agg2_ref, slope_ref, turned_ref, w1_out, w2_out, cot_ref, sem, *, groups
):
    copy = pltpu.make_async_copy(cot_hbm.at[0], cot_ref, sem)
    copy.start()
    hidden = w2_ref.shape[0]
    depth = hidden // groups
    target = lax.broadcasted_iota(jnp.int32, (hidden, hidden), 0)
    source = lax.broadcasted_iota(jnp.int32, (hidden, hidden), 1)
    plane = (target % depth + DEPTH_FIRST) % depth
    place = (target // depth + PLANE_FIRST) % groups
    order = (source == plane * groups + place).astype(jnp.bfloat16)
    w1 = dot(w1_ref[...], order, 1, 1).astype(jnp.bfloat16)
    w1_out[...] = w1
    w2_out[...] = dot(order, w2_ref[...]).astype(jnp.bfloat16)
    value, slope = gelu_parts(dot(own_ref[...], w1))
    slope_ref[...] = slope
    agg2_ref[...] = dot(adj_ref[1], value.astype(jnp.bfloat16))
    nodes = own_ref.shape[0]
    for part in range(3):
        turned_ref[part * nodes : (part + 1) * nodes, :] = adj_ref[part].T
    copy.wait()


def other_kernel(adj_ref, other_ref, w1_ref, near_ref, agg2_ref, slope_ref):
    value, slope = gelu_parts(dot(other_ref[...], w1_ref[...]))
    slope_ref[...] = slope
    agg2_ref[...] = near_ref[...] + dot(adj_ref[2], value.astype(jnp.bfloat16))


def layers_kernel(
    adj_ref, cross_ref, own_ref, other_ref, cot_ref, agg2_ref, own_slope_ref, other_slope_ref, turned_ref,
    w1_ref, w2_ref, out_ref,
):
    nodes, features = own_ref.shape
    cross = cross_ref[:nodes, :]
    value, slope = gelu_parts(dot(cross, w1_ref[...]))
    agg2 = agg2_ref[...] + dot(adj_ref[0], value.astype(jnp.bfloat16))
    agg2 = agg2.astype(jnp.bfloat16)
    unused, slope2 = gelu_parts(dot(agg2, w2_ref[...]))
    dpre2 = (cot_ref[...].astype(jnp.float32) * slope2).astype(jnp.bfloat16)
    dagg2 = dot(dpre2, w2_ref[...], 1, 1).astype(jnp.bfloat16)
    groups, depth = out_ref.shape[0], out_ref.shape[1]
    second = dot(agg2.T, dpre2)
    out_ref[:, :, features:] = second.astype(jnp.bfloat16).reshape(groups, depth, second.shape[1])
    spread = dot(turned_ref[...], dagg2)
    slopes = (slope, own_slope_ref[...], other_slope_ref[...])
    dpre1 = [
        (spread[part * nodes : (part + 1) * nodes] * slope).astype(jnp.bfloat16)
        for part, slope in enumerate(slopes)
    ]
    agg1 = jnp.concatenate([cross, own_ref[...], other_ref[...]], axis=0)
    first = dot(agg1.T, jnp.concatenate(dpre1, axis=0)).astype(jnp.bfloat16).T
    out_ref[:, :, :features] = first.reshape(groups, depth, features)


def depth_sum_kernel(in_ref, first_ref, second_ref):
    total = jnp.sum(in_ref[...].astype(jnp.float32), axis=0)
    pieces = first_ref.shape[1] // 128
    for piece in range(total.shape[0]):
        ref, place = (first_ref, piece) if piece < pieces else (second_ref, piece - pieces)
        ref[:, place * 128 : (place + 1) * 128] = total[piece : piece + 1, :]


def cross_swap(block):
    count = lax.axis_size(SECTION)
    pairs = [(i, i + 1) for i in range(1, count - 1, 2)]
    return lax.ppermute(block, SECTION, pairs + [(j, i) for i, j in pairs])


def core_swap(block):
    return lax.ppermute(block, "c", [(0, 1), (1, 0)])


def body(features, grad_out, w_first, w_second, tile_values, tile_rows, tile_cols, tile_count):
    own = features[0]
    nodes, in_features = own.shape
    hidden = w_second.shape[0]
    depth = lax.axis_size("z")
    plane = lax.axis_size(PLANE)
    odd = lax.axis_index("c").astype(jnp.int32).reshape(1)

    cross = cross_swap(own)
    other = core_swap(own)
    inputs = (tile_rows, tile_cols, tile_values, features)
    adjacency, near = pl.pallas_call(
        adjacency_kernel,
        out_shape=(
            jax.ShapeDtypeStruct((3, nodes, nodes), jnp.bfloat16),
            jax.ShapeDtypeStruct((nodes, in_features), jnp.float32),
        ),
        in_specs=[SMEM] * 2 + [HBM] * 4,
        out_specs=(VMEM, VMEM),
        scratch_shapes=[pltpu.SMEM(i.shape, i.dtype) for i in inputs[:2]]
        + [pltpu.VMEM(i.shape, i.dtype) for i in inputs[2:]]
        + [pltpu.SemaphoreType.DMA((4,))],
        compiler_params=pltpu.CompilerParams(vmem_limit_bytes=4 * MIB),
        name="adjacency",
    )(odd, tile_count, *[pltpu.with_memory_space_constraint(i, pltpu.HBM) for i in inputs])
    agg1, sent = pl.pallas_call(
        aggregate_kernel,
        out_shape=(
            jax.ShapeDtypeStruct((nodes, in_features), jnp.bfloat16),
            jax.ShapeDtypeStruct((nodes + 16, in_features), jnp.bfloat16),
        ),
        in_specs=[VMEM] * 4,
        out_specs=(VMEM, VMEM),
        compiler_params=pltpu.CompilerParams(vmem_limit_bytes=4 * MIB),
        name="aggregate",
    )(other, adjacency, near, cross)

    cross = cross_swap(sent)
    other = core_swap(agg1)
    agg2, own_slope, turned, w_first, w_second, cotangent = pl.pallas_call(
        functools.partial(own_kernel, groups=plane),
        out_shape=(
            jax.ShapeDtypeStruct((nodes, hidden), jnp.float32),
            jax.ShapeDtypeStruct((nodes, hidden), jnp.float32),
            jax.ShapeDtypeStruct((3 * nodes, nodes), jnp.bfloat16),
            jax.ShapeDtypeStruct(w_first.shape, w_first.dtype),
            jax.ShapeDtypeStruct(w_second.shape, w_second.dtype),
            jax.ShapeDtypeStruct((nodes, hidden), grad_out.dtype),
        ),
        in_specs=[VMEM] * 4 + [HBM],
        out_specs=[VMEM] * 6,
        scratch_shapes=[pltpu.SemaphoreType.DMA],
        compiler_params=pltpu.CompilerParams(vmem_limit_bytes=12 * MIB),
        cost_estimate=pl.CostEstimate(flops=600_000_000, bytes_accessed=4 * MIB, transcendentals=131072),
        name="own_part",
    )(adjacency, agg1, w_first, w_second, pltpu.with_memory_space_constraint(grad_out, pltpu.HBM))
    agg2, other_slope = pl.pallas_call(
        other_kernel,
        out_shape=(
            jax.ShapeDtypeStruct((nodes, hidden), jnp.float32),
            jax.ShapeDtypeStruct((nodes, hidden), jnp.float32),
        ),
        in_specs=[VMEM] * 4,
        out_specs=[VMEM] * 2,
        compiler_params=pltpu.CompilerParams(vmem_limit_bytes=8 * MIB),
        name="other_part",
    )(adjacency, other, w_first, agg2)
    gradients = pl.pallas_call(
        layers_kernel,
        out_shape=jax.ShapeDtypeStruct((plane, depth, in_features + hidden), jnp.bfloat16),
        in_specs=[VMEM] * 11,
        out_specs=VMEM,
        compiler_params=pltpu.CompilerParams(vmem_limit_bytes=12 * MIB),
        name="layers",
    )(adjacency, cross, agg1, other, cotangent, agg2, own_slope, other_slope, turned, w_first, w_second)

    groups = [[(i + PLANE_FIRST) % plane for i in range(plane)]]
    gathered = lax.all_to_all(gradients, PLANE, 0, 0, axis_index_groups=groups, tiled=True)
    partial = jnp.sum(gathered.astype(jnp.float32), axis=0)
    partial = partial.astype(jnp.bfloat16).reshape(depth, (in_features + hidden) // 128, 128)
    groups = [[(i + DEPTH_FIRST) % depth for i in range(depth)]]
    collected = lax.all_to_all(partial, "z", 0, 0, axis_index_groups=groups, tiled=True)
    return pl.pallas_call(
        depth_sum_kernel,
        out_shape=(
            jax.ShapeDtypeStruct((1, in_features), jnp.float32),
            jax.ShapeDtypeStruct((1, hidden), jnp.float32),
        ),
        in_specs=[VMEM],
        out_specs=(VMEM, VMEM),
        compiler_params=pltpu.CompilerParams(vmem_limit_bytes=4 * MIB),
        name="depth_sum",
    )(collected)


def solution(mesh):
    fine = Mesh(mesh.devices.reshape(16, 4, 2, 4), ("z", "y", "c", "x"))
    placed = (
        P("x", SECTION, None),
        P("x", SECTION, None),
        P(),
        P(),
        P("x", SECTION, None, None),
        P("x", SECTION),
        P("x", SECTION),
        P("x", SECTION),
    )
    rows = ("z", "y", "c", "x")
    return jax.shard_map(
        body,
        mesh=fine,
        in_specs=placed,
        out_specs=(P(rows, None), P(rows, None)),
        check_vma=False,
    )
```

```python
import functools

import jax
import jax.numpy as jnp
from jax import lax
from jax.experimental import pallas as pl
from jax.experimental.pallas import tpu as pltpu
from jax.sharding import Mesh
from jax.sharding import PartitionSpec as P

TILE = 128
SECTION = ("z", "y", "c")
PLANE = ("y", "c", "x")
SCALE = 0.7978845608028654
CUBIC = 0.044715
MIB = 1024 * 1024
DEPTH_FIRST = 10
PLANE_FIRST = 23
VMEM = pl.BlockSpec(memory_space=pltpu.VMEM)
HBM = pl.BlockSpec(memory_space=pltpu.HBM)
SMEM = pl.BlockSpec(memory_space=pltpu.SMEM)


def dot(lhs, rhs, lhs_dim=1, rhs_dim=0):
    return lax.dot_general(
        lhs, rhs, (((lhs_dim,), (rhs_dim,)), ((), ())), preferred_element_type=jnp.float32
    )


def gelu_parts(v):
    square = v * v
    t = jnp.tanh(v * (SCALE + (SCALE * CUBIC) * square))
    half = 0.5 + 0.5 * t
    slope = half + (0.5 * v) * (1.0 - t * t) * (SCALE + (3.0 * SCALE * CUBIC) * square)
    return v * half, slope


def adjacency_kernel(
    odd_ref, count_ref, rows_hbm, cols_hbm, tiles_hbm, own_hbm, adj_ref, near_ref,
    rows_ref, cols_ref, tiles_ref, own_ref, sems,
):
    pairs = ((rows_hbm, rows_ref), (cols_hbm, cols_ref), (tiles_hbm, tiles_ref), (own_hbm, own_ref))
    copies = [pltpu.make_async_copy(src, dst, sems.at[i]) for i, (src, dst) in enumerate(pairs)]
    for copy in copies:
        copy.start()
    adj_ref[...] = jnp.zeros_like(adj_ref)
    odd = odd_ref[0]
    for copy in copies:
        copy.wait()
    live = count_ref[0, 0]
    for slot in range(tiles_ref.shape[1]):

        @pl.when(slot < live)
        def _():
            row = pl.multiple_of(rows_ref[0, slot] * TILE, TILE)
            col = cols_ref[0, slot]
            side = col // 2
            part = jnp.where(odd == 1, 2 - side, side)
            col = pl.multiple_of((col - 2 * side) * TILE, TILE)
            adj_ref[part, pl.ds(row, TILE), pl.ds(col, TILE)] = tiles_ref[0, slot]

    near_ref[...] = dot(adj_ref[1], own_ref[0])


def aggregate_kernel(other_ref, adj_ref, near_ref, cross_ref, agg1_ref, sent_ref):
    nodes = agg1_ref.shape[0]
    agg1 = near_ref[...] + dot(adj_ref[2], other_ref[...]) + dot(adj_ref[0], cross_ref[...])
    agg1 = agg1.astype(jnp.bfloat16)
    agg1_ref[...] = agg1
    sent_ref[:nodes, :] = agg1
    sent_ref[nodes:, :] = jnp.zeros((sent_ref.shape[0] - nodes, agg1.shape[1]), agg1.dtype)


def own_kernel(
    adj_ref, own_ref, w1_ref, w2_ref, cot_hbm, agg2_ref, slope_ref, turned_ref, w1_out, w2_out, cot_ref, sem, *, groups
):
    copy = pltpu.make_async_copy(cot_hbm.at[0], cot_ref, sem)
    copy.start()
    hidden = w2_ref.shape[0]
    depth = hidden // groups
    target = lax.broadcasted_iota(jnp.int32, (hidden, hidden), 0)
    source = lax.broadcasted_iota(jnp.int32, (hidden, hidden), 1)
    plane = (target % depth + DEPTH_FIRST) % depth
    place = (target // depth + PLANE_FIRST) % groups
    order = (source == plane * groups + place).astype(jnp.bfloat16)
    w1 = dot(w1_ref[...], order, 1, 1).astype(jnp.bfloat16)
    w1_out[...] = w1
    w2_out[...] = dot(order, w2_ref[...]).astype(jnp.bfloat16)
    value, slope = gelu_parts(dot(own_ref[...], w1))
    slope_ref[...] = slope
    agg2_ref[...] = dot(adj_ref[1], value.astype(jnp.bfloat16))
    nodes = own_ref.shape[0]
    for part in range(3):
        turned_ref[part * nodes : (part + 1) * nodes, :] = adj_ref[part].T
    copy.wait()


def other_kernel(adj_ref, other_ref, w1_ref, near_ref, agg2_ref, slope_ref):
    value, slope = gelu_parts(dot(other_ref[...], w1_ref[...]))
    slope_ref[...] = slope
    agg2_ref[...] = near_ref[...] + dot(adj_ref[2], value.astype(jnp.bfloat16))


def layers_kernel(
    adj_ref, cross_ref, own_ref, other_ref, cot_ref, agg2_ref, own_slope_ref, other_slope_ref, turned_ref,
    w1_ref, w2_ref, out_ref,
):
    nodes, features = own_ref.shape
    cross = cross_ref[:nodes, :]
    value, slope = gelu_parts(dot(cross, w1_ref[...]))
    agg2 = agg2_ref[...] + dot(adj_ref[0], value.astype(jnp.bfloat16))
    agg2 = agg2.astype(jnp.bfloat16)
    unused, slope2 = gelu_parts(dot(agg2, w2_ref[...]))
    dpre2 = (cot_ref[...].astype(jnp.float32) * slope2).astype(jnp.bfloat16)
    dagg2 = dot(dpre2, w2_ref[...], 1, 1).astype(jnp.bfloat16)
    groups, depth = out_ref.shape[0], out_ref.shape[1]
    second = dot(agg2.T, dpre2)
    out_ref[:, :, features:] = second.astype(jnp.bfloat16).reshape(groups, depth, second.shape[1])
    spread = dot(turned_ref[...], dagg2)
    slopes = (slope, own_slope_ref[...], other_slope_ref[...])
    dpre1 = [
        (spread[part * nodes : (part + 1) * nodes] * slope).astype(jnp.bfloat16)
        for part, slope in enumerate(slopes)
    ]
    agg1 = jnp.concatenate([cross, own_ref[...], other_ref[...]], axis=0)
    first = dot(agg1.T, jnp.concatenate(dpre1, axis=0)).astype(jnp.bfloat16).T
    out_ref[:, :, :features] = first.reshape(groups, depth, features)


def depth_sum_kernel(in_ref, first_ref, second_ref):
    total = jnp.sum(in_ref[...].astype(jnp.float32), axis=0)
    pieces = first_ref.shape[1] // 128
    for piece in range(total.shape[0]):
        ref, place = (first_ref, piece) if piece < pieces else (second_ref, piece - pieces)
        ref[:, place * 128 : (place + 1) * 128] = total[piece : piece + 1, :]


def cross_swap(block):
    count = lax.axis_size(SECTION)
    pairs = [(i, i + 1) for i in range(1, count - 1, 2)]
    return lax.ppermute(block, SECTION, pairs + [(j, i) for i, j in pairs])


def core_swap(block):
    return lax.ppermute(block, "c", [(0, 1), (1, 0)])


def body(features, grad_out, w_first, w_second, tile_values, tile_rows, tile_cols, tile_count):
    own = features[0]
    nodes, in_features = own.shape
    hidden = w_second.shape[0]
    depth = lax.axis_size("z")
    plane = lax.axis_size(PLANE)
    odd = lax.axis_index("c").astype(jnp.int32).reshape(1)

    cross = cross_swap(own)
    other = core_swap(own)
    inputs = (tile_rows, tile_cols, tile_values, features)
    adjacency, near = pl.pallas_call(
        adjacency_kernel,
        out_shape=(
            jax.ShapeDtypeStruct((3, nodes, nodes), jnp.bfloat16),
            jax.ShapeDtypeStruct((nodes, in_features), jnp.float32),
        ),
        in_specs=[SMEM] * 2 + [HBM] * 4,
        out_specs=(VMEM, VMEM),
        scratch_shapes=[pltpu.SMEM(i.shape, i.dtype) for i in inputs[:2]]
        + [pltpu.VMEM(i.shape, i.dtype) for i in inputs[2:]]
        + [pltpu.SemaphoreType.DMA((4,))],
        compiler_params=pltpu.CompilerParams(vmem_limit_bytes=4 * MIB),
        name="adjacency",
    )(odd, tile_count, *[pltpu.with_memory_space_constraint(i, pltpu.HBM) for i in inputs])
    agg1, sent = pl.pallas_call(
        aggregate_kernel,
        out_shape=(
            jax.ShapeDtypeStruct((nodes, in_features), jnp.bfloat16),
            jax.ShapeDtypeStruct((nodes + 16, in_features), jnp.bfloat16),
        ),
        in_specs=[VMEM] * 4,
        out_specs=(VMEM, VMEM),
        compiler_params=pltpu.CompilerParams(vmem_limit_bytes=4 * MIB),
        name="aggregate",
    )(other, adjacency, near, cross)

    cross = cross_swap(sent)
    other = core_swap(agg1)
    agg2, own_slope, turned, w_first, w_second, cotangent = pl.pallas_call(
        functools.partial(own_kernel, groups=plane),
        out_shape=(
            jax.ShapeDtypeStruct((nodes, hidden), jnp.float32),
            jax.ShapeDtypeStruct((nodes, hidden), jnp.float32),
            jax.ShapeDtypeStruct((3 * nodes, nodes), jnp.bfloat16),
            jax.ShapeDtypeStruct(w_first.shape, w_first.dtype),
            jax.ShapeDtypeStruct(w_second.shape, w_second.dtype),
            jax.ShapeDtypeStruct((nodes, hidden), grad_out.dtype),
        ),
        in_specs=[VMEM] * 4 + [HBM],
        out_specs=[VMEM] * 6,
        scratch_shapes=[pltpu.SemaphoreType.DMA],
        compiler_params=pltpu.CompilerParams(vmem_limit_bytes=12 * MIB),
        cost_estimate=pl.CostEstimate(flops=600_000_000, bytes_accessed=4 * MIB, transcendentals=131072),
        name="own_part",
    )(adjacency, agg1, w_first, w_second, pltpu.with_memory_space_constraint(grad_out, pltpu.HBM))
    agg2, other_slope = pl.pallas_call(
        other_kernel,
        out_shape=(
            jax.ShapeDtypeStruct((nodes, hidden), jnp.float32),
            jax.ShapeDtypeStruct((nodes, hidden), jnp.float32),
        ),
        in_specs=[VMEM] * 4,
        out_specs=[VMEM] * 2,
        compiler_params=pltpu.CompilerParams(vmem_limit_bytes=8 * MIB),
        name="other_part",
    )(adjacency, other, w_first, agg2)
    gradients = pl.pallas_call(
        layers_kernel,
        out_shape=jax.ShapeDtypeStruct((plane, depth, in_features + hidden), jnp.bfloat16),
        in_specs=[VMEM] * 11,
        out_specs=VMEM,
        compiler_params=pltpu.CompilerParams(vmem_limit_bytes=12 * MIB),
        name="layers",
    )(adjacency, cross, agg1, other, cotangent, agg2, own_slope, other_slope, turned, w_first, w_second)

    groups = [[(i + PLANE_FIRST) % plane for i in range(plane)]]
    gathered = lax.all_to_all(gradients, PLANE, 0, 0, axis_index_groups=groups, tiled=True)
    partial = jnp.sum(gathered.astype(jnp.float32), axis=0)
    partial = partial.astype(jnp.bfloat16).reshape(depth, (in_features + hidden) // 128, 128)
    groups = [[(i + DEPTH_FIRST) % depth for i in range(depth)]]
    collected = lax.all_to_all(partial, "z", 0, 0, axis_index_groups=groups, tiled=True)
    return pl.pallas_call(
        depth_sum_kernel,
        out_shape=(
            jax.ShapeDtypeStruct((1, in_features), jnp.float32),
            jax.ShapeDtypeStruct((1, hidden), jnp.float32),
        ),
        in_specs=[VMEM],
        out_specs=(VMEM, VMEM),
        compiler_params=pltpu.CompilerParams(vmem_limit_bytes=4 * MIB),
        name="depth_sum",
    )(collected)


def solution(mesh):
    fine = Mesh(mesh.devices.reshape(16, 4, 2, 4), ("z", "y", "c", "x"))
    placed = (
        P("x", SECTION, None),
        P("x", SECTION, None),
        P(),
        P(),
        P("x", SECTION, None, None),
        P("x", SECTION),
        P("x", SECTION),
        P("x", SECTION),
    )
    rows = ("z", "y", "c", "x")
    return jax.shard_map(
        body,
        mesh=fine,
        in_specs=placed,
        out_specs=(P(rows, None), P(rows, None)),
        check_vma=False,
    )
```

```python
import functools

import jax
import jax.numpy as jnp
from jax import lax
from jax.experimental import pallas as pl
from jax.experimental.pallas import tpu as pltpu
from jax.sharding import Mesh
from jax.sharding import PartitionSpec as P

TILE = 128
SECTION = ("z", "y", "c")
PLANE = ("y", "c", "x")
SCALE = 0.7978845608028654
CUBIC = 0.044715
MIB = 1024 * 1024
DEPTH_FIRST = 11
PLANE_FIRST = 22
VMEM = pl.BlockSpec(memory_space=pltpu.VMEM)
HBM = pl.BlockSpec(memory_space=pltpu.HBM)
SMEM = pl.BlockSpec(memory_space=pltpu.SMEM)


def dot(lhs, rhs, lhs_dim=1, rhs_dim=0):
    return lax.dot_general(
        lhs, rhs, (((lhs_dim,), (rhs_dim,)), ((), ())), preferred_element_type=jnp.float32
    )


def gelu_parts(v):
    square = v * v
    t = jnp.tanh(v * (SCALE + (SCALE * CUBIC) * square))
    half = 0.5 + 0.5 * t
    slope = half + (0.5 * v) * (1.0 - t * t) * (SCALE + (3.0 * SCALE * CUBIC) * square)
    return v * half, slope


def adjacency_kernel(
    odd_ref, count_ref, rows_hbm, cols_hbm, tiles_hbm, own_hbm, adj_ref, near_ref,
    rows_ref, cols_ref, tiles_ref, own_ref, sems,
):
    pairs = ((rows_hbm, rows_ref), (cols_hbm, cols_ref), (tiles_hbm, tiles_ref), (own_hbm, own_ref))
    copies = [pltpu.make_async_copy(src, dst, sems.at[i]) for i, (src, dst) in enumerate(pairs)]
    for copy in copies:
        copy.start()
    adj_ref[...] = jnp.zeros_like(adj_ref)
    odd = odd_ref[0]
    for copy in copies:
        copy.wait()
    live = count_ref[0, 0]
    for slot in range(tiles_ref.shape[1]):

        @pl.when(slot < live)
        def _():
            row = pl.multiple_of(rows_ref[0, slot] * TILE, TILE)
            col = cols_ref[0, slot]
            side = col // 2
            part = jnp.where(odd == 1, 2 - side, side)
            col = pl.multiple_of((col - 2 * side) * TILE, TILE)
            adj_ref[part, pl.ds(row, TILE), pl.ds(col, TILE)] = tiles_ref[0, slot]

    near_ref[...] = dot(adj_ref[1], own_ref[0])


def aggregate_kernel(other_ref, adj_ref, near_ref, cross_ref, agg1_ref, sent_ref):
    nodes = agg1_ref.shape[0]
    agg1 = near_ref[...] + dot(adj_ref[2], other_ref[...]) + dot(adj_ref[0], cross_ref[...])
    agg1 = agg1.astype(jnp.bfloat16)
    agg1_ref[...] = agg1
    sent_ref[:nodes, :] = agg1
    sent_ref[nodes:, :] = jnp.zeros((sent_ref.shape[0] - nodes, agg1.shape[1]), agg1.dtype)


def own_kernel(
    adj_ref, own_ref, w1_ref, w2_ref, cot_hbm, agg2_ref, slope_ref, turned_ref, w1_out, w2_out, cot_ref, sem, *, groups
):
    copy = pltpu.make_async_copy(cot_hbm.at[0], cot_ref, sem)
    copy.start()
    hidden = w2_ref.shape[0]
    depth = hidden // groups
    target = lax.broadcasted_iota(jnp.int32, (hidden, hidden), 0)
    source = lax.broadcasted_iota(jnp.int32, (hidden, hidden), 1)
    plane = (target % depth + DEPTH_FIRST) % depth
    place = (target // depth + PLANE_FIRST) % groups
    order = (source == plane * groups + place).astype(jnp.bfloat16)
    w1 = dot(w1_ref[...], order, 1, 1).astype(jnp.bfloat16)
    w1_out[...] = w1
    w2_out[...] = dot(order, w2_ref[...]).astype(jnp.bfloat16)
    value, slope = gelu_parts(dot(own_ref[...], w1))
    slope_ref[...] = slope
    agg2_ref[...] = dot(adj_ref[1], value.astype(jnp.bfloat16))
    nodes = own_ref.shape[0]
    for part in range(3):
        turned_ref[part * nodes : (part + 1) * nodes, :] = adj_ref[part].T
    copy.wait()


def other_kernel(adj_ref, other_ref, w1_ref, near_ref, agg2_ref, slope_ref):
    value, slope = gelu_parts(dot(other_ref[...], w1_ref[...]))
    slope_ref[...] = slope
    agg2_ref[...] = near_ref[...] + dot(adj_ref[2], value.astype(jnp.bfloat16))


def layers_kernel(
    adj_ref, cross_ref, own_ref, other_ref, cot_ref, agg2_ref, own_slope_ref, other_slope_ref, turned_ref,
    w1_ref, w2_ref, out_ref,
):
    nodes, features = own_ref.shape
    cross = cross_ref[:nodes, :]
    value, slope = gelu_parts(dot(cross, w1_ref[...]))
    agg2 = agg2_ref[...] + dot(adj_ref[0], value.astype(jnp.bfloat16))
    agg2 = agg2.astype(jnp.bfloat16)
    unused, slope2 = gelu_parts(dot(agg2, w2_ref[...]))
    dpre2 = (cot_ref[...].astype(jnp.float32) * slope2).astype(jnp.bfloat16)
    dagg2 = dot(dpre2, w2_ref[...], 1, 1).astype(jnp.bfloat16)
    groups, depth = out_ref.shape[0], out_ref.shape[1]
    second = dot(agg2.T, dpre2)
    out_ref[:, :, features:] = second.astype(jnp.bfloat16).reshape(groups, depth, second.shape[1])
    spread = dot(turned_ref[...], dagg2)
    slopes = (slope, own_slope_ref[...], other_slope_ref[...])
    dpre1 = [
        (spread[part * nodes : (part + 1) * nodes] * slope).astype(jnp.bfloat16)
        for part, slope in enumerate(slopes)
    ]
    agg1 = jnp.concatenate([cross, own_ref[...], other_ref[...]], axis=0)
    first = dot(agg1.T, jnp.concatenate(dpre1, axis=0)).astype(jnp.bfloat16).T
    out_ref[:, :, :features] = first.reshape(groups, depth, features)


def depth_sum_kernel(in_ref, first_ref, second_ref):
    total = jnp.sum(in_ref[...].astype(jnp.float32), axis=0)
    pieces = first_ref.shape[1] // 128
    for piece in range(total.shape[0]):
        ref, place = (first_ref, piece) if piece < pieces else (second_ref, piece - pieces)
        ref[:, place * 128 : (place + 1) * 128] = total[piece : piece + 1, :]


def cross_swap(block):
    count = lax.axis_size(SECTION)
    pairs = [(i, i + 1) for i in range(1, count - 1, 2)]
    return lax.ppermute(block, SECTION, pairs + [(j, i) for i, j in pairs])


def core_swap(block):
    return lax.ppermute(block, "c", [(0, 1), (1, 0)])


def body(features, grad_out, w_first, w_second, tile_values, tile_rows, tile_cols, tile_count):
    own = features[0]
    nodes, in_features = own.shape
    hidden = w_second.shape[0]
    depth = lax.axis_size("z")
    plane = lax.axis_size(PLANE)
    odd = lax.axis_index("c").astype(jnp.int32).reshape(1)

    cross = cross_swap(own)
    other = core_swap(own)
    inputs = (tile_rows, tile_cols, tile_values, features)
    adjacency, near = pl.pallas_call(
        adjacency_kernel,
        out_shape=(
            jax.ShapeDtypeStruct((3, nodes, nodes), jnp.bfloat16),
            jax.ShapeDtypeStruct((nodes, in_features), jnp.float32),
        ),
        in_specs=[SMEM] * 2 + [HBM] * 4,
        out_specs=(VMEM, VMEM),
        scratch_shapes=[pltpu.SMEM(i.shape, i.dtype) for i in inputs[:2]]
        + [pltpu.VMEM(i.shape, i.dtype) for i in inputs[2:]]
        + [pltpu.SemaphoreType.DMA((4,))],
        compiler_params=pltpu.CompilerParams(vmem_limit_bytes=4 * MIB),
        name="adjacency",
    )(odd, tile_count, *[pltpu.with_memory_space_constraint(i, pltpu.HBM) for i in inputs])
    agg1, sent = pl.pallas_call(
        aggregate_kernel,
        out_shape=(
            jax.ShapeDtypeStruct((nodes, in_features), jnp.bfloat16),
            jax.ShapeDtypeStruct((nodes + 16, in_features), jnp.bfloat16),
        ),
        in_specs=[VMEM] * 4,
        out_specs=(VMEM, VMEM),
        compiler_params=pltpu.CompilerParams(vmem_limit_bytes=4 * MIB),
        name="aggregate",
    )(other, adjacency, near, cross)

    cross = cross_swap(sent)
    other = core_swap(agg1)
    agg2, own_slope, turned, w_first, w_second, cotangent = pl.pallas_call(
        functools.partial(own_kernel, groups=plane),
        out_shape=(
            jax.ShapeDtypeStruct((nodes, hidden), jnp.float32),
            jax.ShapeDtypeStruct((nodes, hidden), jnp.float32),
            jax.ShapeDtypeStruct((3 * nodes, nodes), jnp.bfloat16),
            jax.ShapeDtypeStruct(w_first.shape, w_first.dtype),
            jax.ShapeDtypeStruct(w_second.shape, w_second.dtype),
            jax.ShapeDtypeStruct((nodes, hidden), grad_out.dtype),
        ),
        in_specs=[VMEM] * 4 + [HBM],
        out_specs=[VMEM] * 6,
        scratch_shapes=[pltpu.SemaphoreType.DMA],
        compiler_params=pltpu.CompilerParams(vmem_limit_bytes=12 * MIB),
        cost_estimate=pl.CostEstimate(flops=600_000_000, bytes_accessed=4 * MIB, transcendentals=131072),
        name="own_part",
    )(adjacency, agg1, w_first, w_second, pltpu.with_memory_space_constraint(grad_out, pltpu.HBM))
    agg2, other_slope = pl.pallas_call(
        other_kernel,
        out_shape=(
            jax.ShapeDtypeStruct((nodes, hidden), jnp.float32),
            jax.ShapeDtypeStruct((nodes, hidden), jnp.float32),
        ),
        in_specs=[VMEM] * 4,
        out_specs=[VMEM] * 2,
        compiler_params=pltpu.CompilerParams(vmem_limit_bytes=8 * MIB),
        name="other_part",
    )(adjacency, other, w_first, agg2)
    gradients = pl.pallas_call(
        layers_kernel,
        out_shape=jax.ShapeDtypeStruct((plane, depth, in_features + hidden), jnp.bfloat16),
        in_specs=[VMEM] * 11,
        out_specs=VMEM,
        compiler_params=pltpu.CompilerParams(vmem_limit_bytes=12 * MIB),
        name="layers",
    )(adjacency, cross, agg1, other, cotangent, agg2, own_slope, other_slope, turned, w_first, w_second)

    groups = [[(i + PLANE_FIRST) % plane for i in range(plane)]]
    gathered = lax.all_to_all(gradients, PLANE, 0, 0, axis_index_groups=groups, tiled=True)
    partial = jnp.sum(gathered.astype(jnp.float32), axis=0)
    partial = partial.astype(jnp.bfloat16).reshape(depth, (in_features + hidden) // 128, 128)
    groups = [[(i + DEPTH_FIRST) % depth for i in range(depth)]]
    collected = lax.all_to_all(partial, "z", 0, 0, axis_index_groups=groups, tiled=True)
    return pl.pallas_call(
        depth_sum_kernel,
        out_shape=(
            jax.ShapeDtypeStruct((1, in_features), jnp.float32),
            jax.ShapeDtypeStruct((1, hidden), jnp.float32),
        ),
        in_specs=[VMEM],
        out_specs=(VMEM, VMEM),
        compiler_params=pltpu.CompilerParams(vmem_limit_bytes=4 * MIB),
        name="depth_sum",
    )(collected)


def solution(mesh):
    fine = Mesh(mesh.devices.reshape(16, 4, 2, 4), ("z", "y", "c", "x"))
    placed = (
        P("x", SECTION, None),
        P("x", SECTION, None),
        P(),
        P(),
        P("x", SECTION, None, None),
        P("x", SECTION),
        P("x", SECTION),
        P("x", SECTION),
    )
    rows = ("z", "y", "c", "x")
    return jax.shard_map(
        body,
        mesh=fine,
        in_specs=placed,
        out_specs=(P(rows, None), P(rows, None)),
        check_vma=False,
    )
```
